256 devices in a mesh: tile: 32 (over z, y), batch: 8 (over x, core).
Axes of the slice: x: 4, y: 4, z: 8, core: 2. Of those that a mesh axis runs over, the one named last changes fastest.
Arguments:
- object_field: float32 [2, 8192, 512], P(None, 'tile'), may hold values from -5 to 5
- probe_modes: float32 [4, 2, 256, 256], replicated, may hold values from -4 to 4
- amplitudes: float32 [256, 256, 256], P(('tile', 'batch')), may hold values from 0.2 to 4
- positions: int32 [256, 2], P(('tile', 'batch')), may hold values from 0 to 7936, as said below
- shifts: float32 [256, 2], P(('tile', 'batch')), may hold values from -0.5 to 0.5
Outputs:
- new_object: float32 [2, 8192, 512], P(None, 'tile')
- probe_direction: float32 [4, 2, 256, 256], replicated
- shift_grad: float32 [256, 2], P(('tile', 'batch'))
The draws below stay inside these ranges and needn't reach their ends.
Inputs may be any that keep to these rules, and one draw needn't show every extreme that they name: `positions`: pattern p's corner row lies in strip p // 8, that is from 256 * (p // 8) to that plus 256 - 1, but never past 8192 - 256; its corner column is at most 256, so every patch lies inside the object.
All inputs are finite; a program needn't handle non-finite values.
Results may differ from the reference program's by a relative error of at most 0.0003.
Values sent between devices are 32-bit elements; how exact they have to be, the bound alone decides.
No kernel may reach another device: no remote copies, remote signals or barrier semaphores. Data moves between devices by JAX's collectives and lax.ppermute only.
A program may use at most 128 MiB of HBM per device.

```python
import math
import jax
import jax.numpy as jnp
from jax import lax

P_SIZE = 256
MODES = 4
STRIP = 256
OW = 512
OH = 8192
PAT_STRIP = 8
PATTERNS = 256


def draw_positions(key, part):
    key = jax.random.fold_in(key, 7)
    row_key, col_key = jax.random.split(key)
    indices = jnp.arange(PATTERNS)
    offsets = jax.random.randint(row_key, (PATTERNS,), 0, STRIP)
    offsets = jnp.where(indices == PATTERNS - 1, STRIP - 1, offsets)
    rows = jnp.minimum(indices // PAT_STRIP * STRIP + offsets, OH - P_SIZE)
    columns = jax.random.randint(col_key, (PATTERNS,), 0, OW - P_SIZE + 1)
    columns = jnp.where(indices == 0, OW - P_SIZE, columns)
    columns = jnp.where(indices == PATTERNS - 2, 0, columns)
    rows = jnp.where(indices == 0, 0, rows)
    return jnp.stack([rows, columns], axis=1).astype(jnp.int32)


def levels(stream_key, shape, cuts, least, top_value):
    gain, own = 1.0, jax.random.fold_in(stream_key, 6)
    for axis_at, shards_of in cuts:
        draws = jnp.exp(jax.random.uniform(jax.random.fold_in(own, axis_at), (shards_of,), jnp.float32, least / len(cuts), top_value / len(cuts)))
        gain = gain * jnp.repeat(draws, shape[axis_at] // shards_of).reshape([-1 if axis == axis_at else 1 for axis in range(len(shape))])
    return gain


def centred(rng, extent, scale, bound, pieces=(), kind=jnp.bfloat16):
    drawn = jax.random.normal(rng, extent, jnp.float32) * scale
    if len(pieces) > 0:
        drawn = levels(rng, extent, pieces, -0.22, 0.18) * drawn
    return jnp.clip(drawn, min=-bound, max=bound).astype(kind)


def setup_inputs(seed: int = 0) -> dict:
    key_list = jax.random.split(jax.random.key(seed), 6)
    return {
        "object_field": centred(key_list[0], (2, OH, OW), 0.7, 5.0, ((1, 32),), jnp.float32),
        "probe_modes": centred(key_list[1], (MODES, 2, P_SIZE, P_SIZE), 0.5, 4.0, (), jnp.float32),
        "amplitudes": jnp.clip(jnp.exp(math.log(4.0) - 2.9957323 * jax.random.uniform(key_list[2], (PATTERNS, P_SIZE, P_SIZE), jnp.float32) ** levels(key_list[2], (PATTERNS, P_SIZE, P_SIZE), ((0, 256),), -0.2, 0.2)), 0.2, 4.0),
        "positions": draw_positions(jax.random.fold_in(key_list[5], 71), 0),
        "shifts": jnp.clip(jax.random.uniform(key_list[4], (PATTERNS, 2), jnp.float32, -0.5, 0.5) * levels(key_list[4], (PATTERNS, 2), ((0, 256),), -0.4, 0.0), -0.5, 0.5),
    }


full_turn = 2.0 * math.pi
amplitude_floor = 0.5

def frequencies(count):
    indices = jnp.arange(count)
    return ((indices + count // 2) % count - count // 2).astype(jnp.float32) / count

def forward(field):
    return jnp.fft.fft2(field, norm='ortho')

def backward(field):
    return jnp.fft.ifft2(field, norm='ortho')

def squared(field):
    return jnp.real(field) * jnp.real(field) + jnp.imag(field) * jnp.imag(field)

def reference(object_field, probe_modes, amplitudes, positions, shifts):
    frequency = frequencies(P_SIZE)
    probe_hat = forward(probe_modes[:, 0] + 1j * probe_modes[:, 1])
    object_complex = object_field[0] + 1j * object_field[1]

    def visit(carry, pattern_item):
        numerator, weights, grad_hat, mass = carry
        measured, corner, shift_pair = pattern_item
        row_start = corner[0].astype(jnp.int32)
        col_start = corner[1].astype(jnp.int32)
        patch = lax.dynamic_slice(object_complex, (row_start, col_start), (P_SIZE, P_SIZE))
        phase_angle = -full_turn * (shift_pair[0] * frequency[:, None] + shift_pair[1] * frequency[None, :])
        ramp_field = jnp.cos(phase_angle) + 1j * jnp.sin(phase_angle)
        spectrum = ramp_field[None] * probe_hat
        shifted = backward(spectrum)
        exit_wave = shifted * patch[None]
        far_field = forward(exit_wave)
        intensity = lax.optimization_barrier(jnp.sum(squared(far_field), axis=0))
        ratio = measured / jnp.maximum(jnp.sqrt(intensity), amplitude_floor)
        change = backward(far_field * ratio[None]) - exit_wave
        num_term = lax.optimization_barrier(jnp.sum(jnp.conj(shifted) * change, axis=0))
        weight_term = lax.optimization_barrier(jnp.sum(squared(shifted), axis=0))
        chi_hat = forward(jnp.conj(patch)[None] * change)
        cross = lax.optimization_barrier(jnp.sum(jnp.imag(jnp.conj(chi_hat) * spectrum), axis=0))
        grad_pair = full_turn / P_SIZE * jnp.stack([jnp.sum(frequency[:, None] * cross), jnp.sum(frequency[None, :] * cross)])
        grad_hat = grad_hat + jnp.conj(ramp_field)[None] * chi_hat
        mass = mass + squared(patch)
        old_num = lax.dynamic_slice(numerator, (row_start, col_start), (P_SIZE, P_SIZE))
        numerator = lax.dynamic_update_slice(numerator, old_num + num_term, (row_start, col_start))
        old_weight = lax.dynamic_slice(weights, (row_start, col_start), (P_SIZE, P_SIZE))
        weights = lax.dynamic_update_slice(weights, old_weight + weight_term, (row_start, col_start))
        return ((numerator, weights, grad_hat, mass), grad_pair)
    start_carry = (jnp.zeros(object_complex.shape, object_complex.dtype), jnp.zeros(object_field.shape[1:], jnp.float32), jnp.zeros(probe_hat.shape, probe_hat.dtype), jnp.zeros((P_SIZE, P_SIZE), jnp.float32))
    final_carry, shift_grad = lax.scan(visit, start_carry, (amplitudes, positions, shifts))
    numerator, weights, grad_hat, mass = final_carry
    update = numerator / (weights + 1.0)
    new_object = object_field + jnp.stack([jnp.real(update), jnp.imag(update)])
    grad_field = backward(grad_hat)
    direction = jnp.stack([jnp.real(grad_field), jnp.imag(grad_field)], axis=1) / jnp.sqrt(mass + 1.0)[None, None]
    return (new_object, direction, shift_grad)
```

```python
import math

import jax
import jax.numpy as jnp
import ml_dtypes
import numpy as np
from jax import lax
from jax.experimental import pallas as pl
from jax.experimental.pallas import tpu as pltpu
from jax.sharding import Mesh
from jax.sharding import PartitionSpec as P

SIDE = 256
MODES = 4
WIDE = 2 * SIDE
full_turn = 2.0 * math.pi
amplitude_floor = 0.5
bf16 = jnp.bfloat16
f32 = jnp.float32

AXES = (("z", 8), ("y", 4), ("x", 4), ("c", 2))
TILE = ("z", "y")
BATCH = ("x", "c")
OWNERS = 8
ROWS = SIDE // OWNERS
PLANE = ("y", "x")
PARTS = 16


def numpy_split(matrix):
    high = matrix.astype(ml_dtypes.bfloat16)
    low = (matrix - high.astype(np.float64)).astype(ml_dtypes.bfloat16)
    return high, low


def right_block(real, imag):
    return np.block([[real, imag], [-imag, real]])


def left_block(real, imag):
    return np.block([[real, -imag], [imag, real]])


def right_three(real, imag):
    high, low = numpy_split(right_block(real, imag))
    return np.concatenate([high, high, low], axis=0)


def left_three(real, imag):
    high, low = numpy_split(left_block(real, imag))
    return np.concatenate([high, high, low], axis=1)


def tables():
    idx = np.arange(SIDE)
    forward = np.exp(-2j * np.pi * (idx[:, None] * idx[None, :] % SIDE) / SIDE) / math.sqrt(SIDE)
    backward = np.conj(forward)
    freq = (((idx + SIDE // 2) % SIDE) - SIDE // 2) / SIDE
    along_rows = backward @ (freq[:, None] * forward)
    along_cols = forward @ (freq[:, None] * backward)
    return forward, backward, along_rows, along_cols


def split(value):
    high = value.astype(bf16)
    low = (value - high.astype(f32)).astype(bf16)
    return high, low


def put_right(stage, row, real, imag):
    rows = slice(row, row + SIDE)
    for at, part in enumerate((real, imag)):
        high, low = split(part)
        stage[rows, at * SIDE : (at + 1) * SIDE] = high
        stage[rows, WIDE + at * SIDE : WIDE + (at + 1) * SIDE] = low
        stage[rows, 2 * WIDE + at * SIDE : 2 * WIDE + (at + 1) * SIDE] = high


def put_left(stage, col, real, imag):
    cols = slice(col, col + SIDE)
    for at, part in enumerate((real, imag)):
        high, low = split(part)
        stage[at * SIDE : (at + 1) * SIDE, cols] = high
        stage[WIDE + at * SIDE : WIDE + (at + 1) * SIDE, cols] = low
        stage[2 * WIDE + at * SIDE : 2 * WIDE + (at + 1) * SIDE, cols] = high


def product(left, right):
    return jnp.dot(left, right, preferred_element_type=f32)


def probe_kernel(
    corner_ref,
    shift_ref,
    probe_ref,
    fwd_real_ref,
    fwd_imag_ref,
    right_fwd_ref,
    right_bwd_ref,
    left_slope_ref,
    right_slope_ref,
    shifted_ref,
    slope_rows_ref,
    slope_cols_ref,
    left_adjoint_ref,
    right_adjoint_ref,
    stage,
    stage_left,
    wide,
    tall,
    left_shift,
    right_shift,
):
    lane = lax.broadcasted_iota(jnp.int32, (1, SIDE), 1)
    freq = (((lane + SIDE // 2) & (SIDE - 1)) - SIDE // 2).astype(f32) / SIDE

    def ramp(offset, shift):
        whole = ((offset * lane) & (SIDE - 1)).astype(f32) / SIDE
        turns = whole + shift * freq
        angle = -full_turn * (turns - jnp.floor(turns + 0.5))
        return jnp.cos(angle), jnp.sin(angle)

    rows_real, rows_imag = ramp(corner_ref[0, 0], shift_ref[0, 0])
    cols_real, cols_imag = ramp(corner_ref[0, 1], shift_ref[0, 1])
    fwd_real = fwd_real_ref[...]
    fwd_imag = fwd_imag_ref[...]
    for at, (real, imag, sign) in enumerate(
        (
            (rows_real, rows_imag, -1.0),
            (rows_real, -rows_imag, -1.0),
            (cols_real, cols_imag, 1.0),
            (cols_real, -cols_imag, 1.0),
        )
    ):
        mat_imag = sign * fwd_imag
        put_right(
            stage,
            at * SIDE,
            fwd_real * real - mat_imag * imag,
            fwd_real * imag + mat_imag * real,
        )
    wide[: 2 * SIDE] = product(stage[: 2 * SIDE], right_fwd_ref[...])
    wide[2 * SIDE :] = product(stage[2 * SIDE :], right_bwd_ref[...])

    def store_left(target, row):
        for at in range(2):
            high, low = split(wide[row : row + SIDE, at * SIDE : (at + 1) * SIDE])
            for third, part in enumerate((high, high, low)):
                base = third * WIDE
                if at == 0:
                    target[:SIDE, base : base + SIDE] = part
                    target[SIDE:, base + SIDE : base + WIDE] = part
                else:
                    target[SIDE:, base : base + SIDE] = part
                    target[:SIDE, base + SIDE : base + WIDE] = -part

    def store_right(target, row):
        for at in range(2):
            high, low = split(wide[row : row + SIDE, at * SIDE : (at + 1) * SIDE])
            for third, part in enumerate((high, high, low)):
                base = third * WIDE
                if at == 0:
                    target[base : base + SIDE, :SIDE] = part
                    target[base + SIDE : base + WIDE, SIDE:] = part
                else:
                    target[base : base + SIDE, SIDE:] = part
                    target[base + SIDE : base + WIDE, :SIDE] = -part

    store_left(left_shift, 0)
    store_left(left_adjoint_ref, SIDE)
    store_right(right_shift, 2 * SIDE)
    store_right(right_adjoint_ref, 3 * SIDE)

    for k in range(MODES):
        put_right(stage, k * SIDE, probe_ref[k, 0], probe_ref[k, 1])
        put_left(stage_left, k * SIDE, probe_ref[k, 0], probe_ref[k, 1])
    tall[...] = product(left_slope_ref[...], stage_left[...])
    for k in range(MODES):
        slope_rows_ref[k, 0] = tall[:SIDE, k * SIDE : (k + 1) * SIDE]
        slope_rows_ref[k, 1] = tall[SIDE:, k * SIDE : (k + 1) * SIDE]
    wide[...] = product(stage[...], right_slope_ref[...])
    for k in range(MODES):
        slope_cols_ref[k, 0] = wide[k * SIDE : (k + 1) * SIDE, :SIDE]
        slope_cols_ref[k, 1] = wide[k * SIDE : (k + 1) * SIDE, SIDE:]
    wide[...] = product(stage[...], right_shift[...])
    for k in range(MODES):
        rows = slice(k * SIDE, (k + 1) * SIDE)
        put_left(stage_left, k * SIDE, wide[rows, :SIDE], wide[rows, SIDE:])
    tall[...] = product(left_shift[...], stage_left[...])
    for k in range(MODES):
        shifted_ref[k, 0] = tall[:SIDE, k * SIDE : (k + 1) * SIDE]
        shifted_ref[k, 1] = tall[SIDE:, k * SIDE : (k + 1) * SIDE]


def pattern_kernel(
    corner_ref,
    core_ref,
    object_ref,
    near_ref,
    far_ref,
    amplitude_ref,
    shifted_ref,
    slope_rows_ref,
    slope_cols_ref,
    left_fwd_ref,
    right_fwd_ref,
    left_adjoint_ref,
    right_adjoint_ref,
    block_ref,
    keep_ref,
    send_ref,
    shift_grad_ref,
    stage,
    stage_left,
    wide,
    tall,
    exit_wave,
    patch,
    grads,
):
    core = core_ref[0, 0]
    row_start = corner_ref[0, 0] & (SIDE - 1)
    col_start = corner_ref[0, 1]
    half = SIDE // 2
    row_at = lax.broadcasted_iota(jnp.int32, (SIDE, SIDE), 0)
    col_at = lax.broadcasted_iota(jnp.int32, (SIDE, SIDE), 1)
    here = row_at >= row_start
    left = col_at >= col_start
    first = core == 0
    for part in range(2):
        own = jnp.where(left, object_ref[part, :, :SIDE], object_ref[part, :, SIDE:])
        near = near_ref[part]
        far = far_ref[part]
        rim = jnp.concatenate([jnp.where(first, near, far), jnp.where(first, far, near)], axis=0)
        rim = jnp.where(left, rim[:, :SIDE], rim[:, SIDE:])
        patch[part] = jnp.where(here, own, rim)

    for k in range(MODES):
        real, imag = shifted_ref[k, 0], shifted_ref[k, 1]
        exit_real = real * patch[0] - imag * patch[1]
        exit_imag = real * patch[1] + imag * patch[0]
        exit_wave[k, 0] = exit_real
        exit_wave[k, 1] = exit_imag
        put_right(stage, k * SIDE, exit_real, exit_imag)
    wide[...] = product(stage[...], right_fwd_ref[...])
    for k in range(MODES):
        rows = slice(k * SIDE, (k + 1) * SIDE)
        put_left(stage_left, k * SIDE, wide[rows, :SIDE], wide[rows, SIDE:])
    tall[...] = product(left_fwd_ref[...], stage_left[...])
    intensity = jnp.zeros((SIDE, SIDE), f32)
    for k in range(MODES):
        cols = slice(k * SIDE, (k + 1) * SIDE)
        real, imag = tall[:SIDE, cols], tall[SIDE:, cols]
        intensity = intensity + (real * real + imag * imag)
    ratio = amplitude_ref[0] / jnp.maximum(jnp.sqrt(intensity), amplitude_floor)
    for k in range(MODES):
        cols = slice(k * SIDE, (k + 1) * SIDE)
        put_left(stage_left, k * SIDE, tall[:SIDE, cols] * ratio, -(tall[SIDE:, cols] * ratio))
    tall[...] = product(left_fwd_ref[...], stage_left[...])
    for k in range(MODES):
        cols = slice(k * SIDE, (k + 1) * SIDE)
        put_right(stage, k * SIDE, tall[:SIDE, cols], tall[SIDE:, cols])
    wide[...] = product(stage[...], right_fwd_ref[...])

    num_real = jnp.zeros((SIDE, SIDE), f32)
    num_imag = jnp.zeros((SIDE, SIDE), f32)
    weight = jnp.zeros((SIDE, SIDE), f32)
    for k in range(MODES):
        rows = slice(k * SIDE, (k + 1) * SIDE)
        real, imag = shifted_ref[k, 0], shifted_ref[k, 1]
        change_real = wide[rows, :SIDE] - exit_wave[k, 0]
        change_imag = -wide[rows, SIDE:] - exit_wave[k, 1]
        num_real = num_real + (real * change_real + imag * change_imag)
        num_imag = num_imag + (real * change_imag - imag * change_real)
        weight = weight + (real * real + imag * imag)
        put_right(
            stage,
            k * SIDE,
            patch[0] * change_real + patch[1] * change_imag,
            patch[0] * change_imag - patch[1] * change_real,
        )
    tag = jnp.where(
        lax.broadcasted_iota(jnp.int32, (8, SIDE), 0) == 0, row_start, col_start
    ).astype(f32)
    for owner in range(OWNERS):
        rows = slice(owner * ROWS, (owner + 1) * ROWS)
        block_ref[owner, :ROWS] = num_real[rows]
        block_ref[owner, ROWS : 2 * ROWS] = num_imag[rows]
        block_ref[owner, 2 * ROWS : 3 * ROWS] = weight[rows]
        block_ref[owner, 3 * ROWS :] = tag

    wide[...] = product(stage[...], right_adjoint_ref[...])
    for k in range(MODES):
        rows = slice(k * SIDE, (k + 1) * SIDE)
        put_left(stage_left, k * SIDE, wide[rows, :SIDE], wide[rows, SIDE:])
    tall[...] = product(left_adjoint_ref[...], stage_left[...])
    row_dot = jnp.zeros((SIDE, SIDE), f32)
    col_dot = jnp.zeros((SIDE, SIDE), f32)
    for k in range(MODES):
        cols = slice(k * SIDE, (k + 1) * SIDE)
        real, imag = tall[:SIDE, cols], tall[SIDE:, cols]
        row_dot = row_dot + (real * slope_rows_ref[k, 1] - imag * slope_rows_ref[k, 0])
        col_dot = col_dot + (real * slope_cols_ref[k, 1] - imag * slope_cols_ref[k, 0])
        grads[2 * k] = real
        grads[2 * k + 1] = imag
    shift_grad_ref[0, 0] = full_turn / SIDE * jnp.sum(row_dot)
    shift_grad_ref[0, 1] = full_turn / SIDE * jnp.sum(col_dot)
    mass = patch[0] * patch[0] + patch[1] * patch[1]
    mass = pltpu.roll(mass, (SIDE - row_start) & (SIDE - 1), 0)
    grads[2 * MODES] = pltpu.roll(mass, (SIDE - col_start) & (SIDE - 1), 1)
    keep_rows = pl.multiple_of(core * half, half)
    send_rows = pl.multiple_of((1 - core) * half, half)
    for channel in range(2 * MODES + 1):
        for target, base in ((keep_ref, keep_rows), (send_ref, send_rows)):
            value = grads[channel, pl.ds(base, half), :]
            for part in range(PARTS):
                target[part, channel] = value[part * 8 : (part + 1) * 8]


def gather_kernel(owner_ref, blocks_ref, own_ref, spill_ref):
    base = owner_ref[0, 0] * ROWS
    row_at = (base + lax.broadcasted_iota(jnp.int32, (ROWS, SIDE), 0)).astype(f32)
    col_at = lax.broadcasted_iota(jnp.int32, (ROWS, SIDE), 1).astype(f32)
    zero = jnp.zeros((ROWS, SIDE), f32)
    for channel in range(3):
        sums = [zero, zero, zero, zero]
        for sender in range(OWNERS):
            value = blocks_ref[sender, channel * ROWS : (channel + 1) * ROWS]
            here = row_at >= blocks_ref[sender, 3 * ROWS : 3 * ROWS + 1]
            left = col_at >= blocks_ref[sender, 3 * ROWS + 1 : 3 * ROWS + 2]
            value_here = jnp.where(here, value, 0.0)
            value_next = jnp.where(here, 0.0, value)
            sums[0] = sums[0] + jnp.where(left, value_here, 0.0)
            sums[1] = sums[1] + jnp.where(left, 0.0, value_here)
            sums[2] = sums[2] + jnp.where(left, value_next, 0.0)
            sums[3] = sums[3] + jnp.where(left, 0.0, value_next)
        own_ref[channel, :, :SIDE] = sums[0]
        own_ref[channel, :, SIDE:] = sums[1]
        spill_ref[channel, :, :SIDE] = sums[2]
        spill_ref[channel, :, SIDE:] = sums[3]


VMEM = pl.BlockSpec(memory_space=pltpu.VMEM)
SMEM = pl.BlockSpec(memory_space=pltpu.SMEM)
LIMIT = 48 * 1024 * 1024


def on_device(object_field, probe_modes, amplitudes, positions, shifts):
    forward, backward, along_rows, along_cols = tables()
    fwd_real = jnp.asarray(forward.real.astype(np.float32))
    fwd_imag = jnp.asarray(forward.imag.astype(np.float32))
    right_fwd = jnp.asarray(right_three(forward.real, forward.imag))
    right_bwd = jnp.asarray(right_three(backward.real, backward.imag))
    left_fwd = jnp.asarray(left_three(forward.real, forward.imag))
    left_slope = jnp.asarray(left_three(along_rows.real, along_rows.imag))
    right_slope = jnp.asarray(right_three(along_cols.real, along_cols.imag))

    core = lax.axis_index("c")
    owner = lax.axis_index(BATCH)
    tiles = 32
    half = SIDE // 2

    part_rows = lax.dynamic_slice_in_dim(object_field, core * half, half, axis=1)
    near = lax.ppermute(part_rows, TILE, [(i + 1, i) for i in range(tiles - 1)])
    far = lax.ppermute(near, "c", [(0, 1), (1, 0)])

    field = jax.ShapeDtypeStruct((MODES, 2, SIDE, SIDE), f32)
    stages = [
        pltpu.VMEM((MODES * SIDE, 3 * WIDE), bf16),
        pltpu.VMEM((3 * WIDE, MODES * SIDE), bf16),
        pltpu.VMEM((MODES * SIDE, WIDE), f32),
        pltpu.VMEM((WIDE, MODES * SIDE), f32),
    ]
    shifted, slope_rows, slope_cols, left_adjoint, right_adjoint = pl.pallas_call(
        probe_kernel,
        out_shape=(
            field,
            field,
            field,
            jax.ShapeDtypeStruct((WIDE, 3 * WIDE), bf16),
            jax.ShapeDtypeStruct((3 * WIDE, WIDE), bf16),
        ),
        in_specs=[SMEM, SMEM] + [VMEM] * 7,
        out_specs=(VMEM,) * 5,
        scratch_shapes=stages
        + [pltpu.VMEM((WIDE, 3 * WIDE), bf16), pltpu.VMEM((3 * WIDE, WIDE), bf16)],
        compiler_params=pltpu.CompilerParams(vmem_limit_bytes=LIMIT),
        cost_estimate=pl.CostEstimate(
            flops=int(8e9), bytes_accessed=int(1.6e7), transcendentals=2048
        ),
    )(
        positions,
        shifts,
        probe_modes,
        fwd_real,
        fwd_imag,
        right_fwd,
        right_bwd,
        left_slope,
        right_slope,
    )

    blocks, keep, send, shift_grad = pl.pallas_call(
        pattern_kernel,
        out_shape=(
            jax.ShapeDtypeStruct((OWNERS, 3 * ROWS + 8, SIDE), f32),
            jax.ShapeDtypeStruct((PARTS, 2 * MODES + 1, 8, SIDE), f32),
            jax.ShapeDtypeStruct((PARTS, 2 * MODES + 1, 8, SIDE), f32),
            jax.ShapeDtypeStruct((1, 2), f32),
        ),
        in_specs=[SMEM, SMEM] + [VMEM] * 11,
        out_specs=(VMEM, VMEM, VMEM, SMEM),
        scratch_shapes=stages
        + [
            pltpu.VMEM((MODES, 2, SIDE, SIDE), f32),
            pltpu.VMEM((2, SIDE, SIDE), f32),
            pltpu.VMEM((2 * MODES + 1, SIDE, SIDE), f32),
        ],
        compiler_params=pltpu.CompilerParams(vmem_limit_bytes=LIMIT),
        cost_estimate=pl.CostEstimate(
            flops=int(1e10), bytes_accessed=int(2e7), transcendentals=65536
        ),
    )(
        positions,
        jnp.reshape(core, (1, 1)),
        object_field,
        near,
        far,
        amplitudes,
        shifted,
        slope_rows,
        slope_cols,
        left_fwd,
        right_fwd,
        left_adjoint,
        right_adjoint,
    )

    other = lax.ppermute(send, "c", [(0, 1), (1, 0)])
    received = lax.all_to_all(blocks, BATCH, 0, 0)
    own, spill = pl.pallas_call(
        gather_kernel,
        out_shape=(jax.ShapeDtypeStruct((3, ROWS, 2 * SIDE), f32),) * 2,
        in_specs=[SMEM, VMEM],
        out_specs=(VMEM, VMEM),
    )(jnp.reshape(owner, (1, 1)), received)
    spilled = lax.ppermute(spill, TILE, [(i, i + 1) for i in range(tiles - 1)])

    scattered = lax.all_to_all(keep + other, PLANE, 0, 0)
    owned = own + spilled
    strip_part = lax.dynamic_slice_in_dim(object_field, owner * ROWS, ROWS, axis=1)
    new_part = strip_part + owned[:2] / (owned[2] + 1.0)[None]
    new_object = lax.all_gather(new_part, BATCH, axis=1, tiled=True)

    column = jnp.sum(scattered, axis=0)
    columns = lax.all_to_all(jnp.broadcast_to(column[None], (8,) + column.shape), "z", 0, 0)
    total = jnp.sum(columns, axis=0)
    direction = total[: 2 * MODES] / jnp.sqrt(total[2 * MODES] + 1.0)[None]
    spread = lax.all_to_all(jnp.broadcast_to(direction[None], (PARTS,) + direction.shape), PLANE, 0, 0)
    swapped = lax.ppermute(spread, "c", [(0, 1), (1, 0)])
    top = jnp.where(core == 0, spread, swapped)
    bottom = jnp.where(core == 0, swapped, spread)
    rows = jnp.concatenate([top, bottom], axis=0)
    probe_direction = jnp.swapaxes(rows, 0, 1).reshape(MODES, 2, SIDE, SIDE)
    return (new_object, probe_direction, shift_grad)


def solution(mesh):
    names = tuple(name for name, _ in AXES)
    sizes = tuple(size for _, size in AXES)
    slice_mesh = Mesh(np.asarray(mesh.devices).reshape(sizes), names)
    return jax.shard_map(
        on_device,
        mesh=slice_mesh,
        in_specs=(
            P(None, TILE, None),
            P(),
            P(names, None, None),
            P(names, None),
            P(names, None),
        ),
        out_specs=(P(None, TILE, None), P(), P(names, None)),
        check_vma=False,
    )
```

```python
import math

import jax
import jax.numpy as jnp
import numpy as np
from jax import lax
from jax.experimental import pallas as pl
from jax.experimental.pallas import tpu as pltpu
from jax.sharding import Mesh
from jax.sharding import PartitionSpec as P

SIDE = 256
MODES = 4
WIDE = 2 * SIDE
full_turn = 2.0 * math.pi
amplitude_floor = 0.5
bf16 = jnp.bfloat16
f32 = jnp.float32

AXES = (("zh", 4), ("zl", 2), ("y", 4), ("x", 4), ("c", 2))
TILE = ("zh", "zl", "y")
BATCH = ("x", "c")
OWNERS = 8
ROWS = SIDE // OWNERS
PLANE = ("zl", "y", "x")
PARTS = 32
LANES = 128


def tables():
    idx = np.arange(SIDE)
    forward = np.exp(-2j * np.pi * (idx[:, None] * idx[None, :] % SIDE) / SIDE) / math.sqrt(SIDE)
    backward = np.conj(forward)
    freq = (((idx + SIDE // 2) % SIDE) - SIDE // 2) / SIDE
    slope = backward @ (freq[:, None] * forward)
    return forward, slope


def two_parts(matrix):
    return np.stack([matrix.real, matrix.imag]).astype(np.float32)


def split(value):
    high = value.astype(bf16)
    low = (value - high.astype(f32)).astype(bf16)
    return high, low


def put_right(stage, row, real, imag):
    rows = slice(row, row + SIDE)
    for at, part in enumerate((real, imag)):
        high, low = split(part)
        stage[rows, at * SIDE : (at + 1) * SIDE] = high
        stage[rows, WIDE + at * SIDE : WIDE + (at + 1) * SIDE] = low


def put_left(stage, col, real, imag):
    cols = slice(col, col + SIDE)
    for at, part in enumerate((real, imag)):
        high, low = split(part)
        stage[at * SIDE : (at + 1) * SIDE, cols] = high
        stage[WIDE + at * SIDE : WIDE + (at + 1) * SIDE, cols] = low


def from_right(stage, matrix):
    fields = jnp.concatenate([stage[...], stage[:, :WIDE]], axis=1)
    return jnp.dot(fields, matrix[...], preferred_element_type=f32)


def from_left(matrix, stage):
    fields = jnp.concatenate([stage[...], stage[:WIDE]], axis=0)
    return jnp.dot(matrix[...], fields, preferred_element_type=f32)


def fill_left(target, real, imag):
    for at, value in enumerate((real, imag)):
        high, low = split(value)
        for third, part in enumerate((high, high, low)):
            base = third * WIDE
            if at == 0:
                target[:SIDE, base : base + SIDE] = part
                target[SIDE:, base + SIDE : base + WIDE] = part
            else:
                target[SIDE:, base : base + SIDE] = part
                target[:SIDE, base + SIDE : base + WIDE] = -part


def fill_right(target, real, imag):
    for at, value in enumerate((real, imag)):
        high, low = split(value)
        for third, part in enumerate((high, high, low)):
            base = third * WIDE
            if at == 0:
                target[base : base + SIDE, :SIDE] = part
                target[base + SIDE : base + WIDE, SIDE:] = part
            else:
                target[base : base + SIDE, SIDE:] = part
                target[base + SIDE : base + WIDE, :SIDE] = -part


def right_to_left(wide, stage_left):
    for k in range(MODES):
        rows = slice(k * SIDE, (k + 1) * SIDE)
        put_left(stage_left, k * SIDE, wide[rows, :SIDE], wide[rows, SIDE:])


def probe_kernel(
    corner_ref,
    shift_ref,
    probe_ref,
    forward_ref,
    shifted_ref,
    adjoint_ref,
    stage,
    stage_left,
    wide,
    tall,
    matrix_right,
    matrix_left,
):
    lane = lax.broadcasted_iota(jnp.int32, (1, SIDE), 1)
    freq = (((lane + SIDE // 2) & (SIDE - 1)) - SIDE // 2).astype(f32) / SIDE

    def ramp(offset, shift):
        whole = ((offset * lane) & (SIDE - 1)).astype(f32) / SIDE
        turns = whole + shift * freq
        angle = -full_turn * (turns - jnp.floor(turns + 0.5))
        return jnp.cos(angle), jnp.sin(angle)

    rows_real, rows_imag = ramp(corner_ref[0, 0], shift_ref[0, 0])
    cols_real, cols_imag = ramp(corner_ref[0, 1], shift_ref[0, 1])
    fwd_real = forward_ref[0]
    fwd_imag = forward_ref[1]
    for at, (real, imag) in enumerate(
        (
            (rows_real, rows_imag),
            (rows_real, -rows_imag),
            (cols_real, cols_imag),
            (cols_real, -cols_imag),
        )
    ):
        put_right(
            stage,
            at * SIDE,
            fwd_real * real + fwd_imag * imag,
            fwd_real * imag - fwd_imag * real,
        )
    fill_right(matrix_right, fwd_real, fwd_imag)
    wide[...] = from_right(stage, matrix_right)
    fill_left(matrix_left, wide[:SIDE, :SIDE], wide[:SIDE, SIDE:])
    adjoint_ref[0] = wide[SIDE : 2 * SIDE, :SIDE]
    adjoint_ref[1] = wide[SIDE : 2 * SIDE, SIDE:]
    adjoint_ref[2] = wide[2 * SIDE : 3 * SIDE, :SIDE]
    adjoint_ref[3] = -wide[2 * SIDE : 3 * SIDE, SIDE:]
    fill_right(matrix_right, wide[3 * SIDE :, :SIDE], -wide[3 * SIDE :, SIDE:])

    for k in range(MODES):
        put_right(stage, k * SIDE, probe_ref[k, 0], probe_ref[k, 1])
    wide[...] = from_right(stage, matrix_right)
    right_to_left(wide, stage_left)
    tall[...] = from_left(matrix_left, stage_left)
    for k in range(MODES):
        cols = slice(k * SIDE, (k + 1) * SIDE)
        shifted_ref[k, 0] = tall[:SIDE, cols]
        shifted_ref[k, 1] = tall[SIDE:, cols]


def partner(owner, steps, turn):
    return (((owner >> 1) + steps) & 3) * 2 + ((owner & 1) ^ turn)


def place(piece):
    row, lane = piece // 2 * 8, piece % 2 * LANES
    return slice(row, row + 8), slice(lane, lane + LANES)


def scatter(target, channel, value):
    for piece in range(PARTS):
        rows, lanes = place(piece)
        target[piece, channel] = value[rows, lanes]


def pattern_kernel(
    corner_ref,
    owner_ref,
    object_ref,
    near_ref,
    far_ref,
    amplitude_ref,
    shifted_ref,
    forward_ref,
    *rest,
):
    block_refs = rest[:4]
    staged_ref, mass_ref = rest[4:6]
    stage, stage_left, wide, tall, exit_wave, patch, left_fwd, right_fwd, nums = rest[6:]
    fill_right(right_fwd, forward_ref[0], forward_ref[1])
    fill_left(left_fwd, forward_ref[0], forward_ref[1])
    owner = owner_ref[0, 0]
    core = owner & 1
    row_start = corner_ref[0, 0] & (SIDE - 1)
    col_start = corner_ref[0, 1]
    row_at = lax.broadcasted_iota(jnp.int32, (SIDE, SIDE), 0)
    col_at = lax.broadcasted_iota(jnp.int32, (SIDE, SIDE), 1)
    here = row_at >= row_start
    left = col_at >= col_start
    first = core == 0
    for part in range(2):
        own = jnp.where(left, object_ref[part, :, :SIDE], object_ref[part, :, SIDE:])
        near = near_ref[part]
        far = far_ref[part]
        rim = jnp.concatenate([jnp.where(first, near, far), jnp.where(first, far, near)], axis=0)
        rim = jnp.where(left, rim[:, :SIDE], rim[:, SIDE:])
        patch[part] = jnp.where(here, own, rim)

    for k in range(MODES):
        real, imag = shifted_ref[k, 0], shifted_ref[k, 1]
        exit_real = real * patch[0] - imag * patch[1]
        exit_imag = real * patch[1] + imag * patch[0]
        exit_wave[k, 0] = exit_real
        exit_wave[k, 1] = exit_imag
        put_right(stage, k * SIDE, exit_real, exit_imag)
    wide[...] = from_right(stage, right_fwd)
    right_to_left(wide, stage_left)
    tall[...] = from_left(left_fwd, stage_left)
    intensity = jnp.zeros((SIDE, SIDE), f32)
    for k in range(MODES):
        cols = slice(k * SIDE, (k + 1) * SIDE)
        real, imag = tall[:SIDE, cols], tall[SIDE:, cols]
        intensity = intensity + (real * real + imag * imag)
    ratio = amplitude_ref[0] / jnp.maximum(jnp.sqrt(intensity), amplitude_floor)
    for k in range(MODES):
        cols = slice(k * SIDE, (k + 1) * SIDE)
        put_left(stage_left, k * SIDE, tall[:SIDE, cols] * ratio, -(tall[SIDE:, cols] * ratio))
    tall[...] = from_left(left_fwd, stage_left)
    for k in range(MODES):
        cols = slice(k * SIDE, (k + 1) * SIDE)
        put_right(stage, k * SIDE, tall[:SIDE, cols], tall[SIDE:, cols])
    wide[...] = from_right(stage, right_fwd)

    num_real = jnp.zeros((SIDE, SIDE), f32)
    num_imag = jnp.zeros((SIDE, SIDE), f32)
    weight = jnp.zeros((SIDE, SIDE), f32)
    for k in range(MODES):
        rows = slice(k * SIDE, (k + 1) * SIDE)
        real, imag = shifted_ref[k, 0], shifted_ref[k, 1]
        change_real = wide[rows, :SIDE] - exit_wave[k, 0]
        change_imag = -wide[rows, SIDE:] - exit_wave[k, 1]
        num_real = num_real + (real * change_real + imag * change_imag)
        num_imag = num_imag + (real * change_imag - imag * change_real)
        weight = weight + (real * real + imag * imag)
        put_right(
            staged_ref,
            k * SIDE,
            patch[0] * change_real + patch[1] * change_imag,
            patch[0] * change_imag - patch[1] * change_real,
        )
    nums[0] = num_real
    nums[1] = num_imag
    nums[2] = weight
    tag = jnp.where(
        lax.broadcasted_iota(jnp.int32, (8, SIDE), 0) == 0, row_start, col_start
    ).astype(f32)
    for steps, block_ref in enumerate(block_refs):
        for turn in range(2):
            base = pl.multiple_of(partner(owner, steps, turn) * ROWS, ROWS)
            for channel in range(3):
                rows = slice(channel * ROWS, (channel + 1) * ROWS)
                block_ref[turn, rows] = nums[channel, pl.ds(base, ROWS), :]
            block_ref[turn, 3 * ROWS :] = tag
    mass_ref[...] = patch[0] * patch[0] + patch[1] * patch[1]


def adjoint_kernel(
    corner_ref,
    owner_ref,
    staged_ref,
    mass_ref,
    adjoint_ref,
    keep_ref,
    send_ref,
    stage_left,
    wide,
    tall,
    matrix_left,
    matrix_right,
    mass,
):
    core = owner_ref[0, 0] & 1
    row_start = corner_ref[0, 0] & (SIDE - 1)
    col_start = corner_ref[0, 1]
    half = SIDE // 2
    fill_right(matrix_right, adjoint_ref[2], adjoint_ref[3])
    wide[...] = from_right(staged_ref, matrix_right)
    fill_left(matrix_left, adjoint_ref[0], adjoint_ref[1])
    right_to_left(wide, stage_left)
    tall[...] = from_left(matrix_left, stage_left)
    turned = pltpu.roll(mass_ref[...], (SIDE - row_start) & (SIDE - 1), 0)
    mass[...] = pltpu.roll(turned, (SIDE - col_start) & (SIDE - 1), 1)
    for target, at in ((keep_ref, core), (send_ref, 1 - core)):
        base = pl.multiple_of(at * half, half)
        for k in range(MODES):
            cols = slice(k * SIDE, (k + 1) * SIDE)
            for part in range(2):
                rows = pl.multiple_of(base + part * SIDE, half)
                scatter(target, 2 * k + part, tall[pl.ds(rows, half), cols])
        scatter(target, 2 * MODES, mass[pl.ds(base, half), :])


def slope_kernel(
    core_ref,
    probe_ref,
    slope_ref,
    keep_ref,
    send_ref,
    shift_grad_ref,
    stage,
    stage_left,
    wide,
    tall,
    matrix_left,
    matrix_right,
):
    first = core_ref[0, 0] == 0
    slope_real = slope_ref[0]
    slope_imag = slope_ref[1]
    fill_left(matrix_left, slope_real, slope_imag)
    fill_right(matrix_right, slope_real.T, slope_imag.T)
    for k in range(MODES):
        put_right(stage, k * SIDE, probe_ref[k, 0], probe_ref[k, 1])
        put_left(stage_left, k * SIDE, probe_ref[k, 0], probe_ref[k, 1])
    tall[...] = from_left(matrix_left, stage_left)
    wide[...] = from_right(stage, matrix_right)
    row_dot = jnp.zeros((8, LANES), f32)
    col_dot = jnp.zeros((8, LANES), f32)
    for piece in range(2 * PARTS):
        top = piece < PARTS
        rows, lanes = place(piece)
        for k in range(MODES):
            kept = [keep_ref[piece % PARTS, 2 * k + part] for part in range(2)]
            sent = [send_ref[piece % PARTS, 2 * k + part] for part in range(2)]
            real, imag = [
                jnp.where(first, a, b) if top else jnp.where(first, b, a)
                for a, b in zip(kept, sent)
            ]
            down = slice(rows.start + SIDE, rows.stop + SIDE)
            over = slice(lanes.start + k * SIDE, lanes.stop + k * SIDE)
            across = slice(rows.start + k * SIDE, rows.stop + k * SIDE)
            wider = slice(lanes.start + SIDE, lanes.stop + SIDE)
            row_dot = row_dot + (real * tall[down, over] - imag * tall[rows, over])
            col_dot = col_dot + (real * wide[across, wider] - imag * wide[across, lanes])
    shift_grad_ref[0, 0] = full_turn / SIDE * jnp.sum(row_dot)
    shift_grad_ref[0, 1] = full_turn / SIDE * jnp.sum(col_dot)


def gather_kernel(owner_ref, *rest):
    own_ref, spill_ref = rest[OWNERS:]
    base = owner_ref[0, 0] * ROWS
    row_at = (base + lax.broadcasted_iota(jnp.int32, (ROWS, SIDE), 0)).astype(f32)
    col_at = lax.broadcasted_iota(jnp.int32, (ROWS, SIDE), 1).astype(f32)
    sums = [[jnp.zeros((ROWS, SIDE), f32) for _ in range(4)] for _ in range(3)]
    for sender in range(OWNERS):
        block_ref = rest[sender].at[sender // 4]
        here = row_at >= block_ref[3 * ROWS : 3 * ROWS + 1]
        left = col_at >= block_ref[3 * ROWS + 1 : 3 * ROWS + 2]
        values = [block_ref[channel * ROWS : (channel + 1) * ROWS] for channel in range(3)]
        for channel, value in enumerate(values):
            value_here = jnp.where(here, value, 0.0)
            value_next = jnp.where(here, 0.0, value)
            terms = (
                jnp.where(left, value_here, 0.0),
                jnp.where(left, 0.0, value_here),
                jnp.where(left, value_next, 0.0),
                jnp.where(left, 0.0, value_next),
            )
            sums[channel] = [total + term for total, term in zip(sums[channel], terms)]
    for channel in range(3):
        own_ref[channel, :, :SIDE] = sums[channel][0]
        own_ref[channel, :, SIDE:] = sums[channel][1]
        spill_ref[channel, :, :SIDE] = sums[channel][2]
        spill_ref[channel, :, SIDE:] = sums[channel][3]


def update_kernel(owner_ref, object_ref, own_ref, spilled_ref, out_ref):
    rows = pl.ds(pl.multiple_of(owner_ref[0, 0] * ROWS, ROWS), ROWS)
    weight = own_ref[2] + spilled_ref[2] + 1.0
    for part in range(2):
        out_ref[part] = object_ref[part, rows, :] + (own_ref[part] + spilled_ref[part]) / weight


def strip_kernel(owner_ref, strip_ref, other_ref, out_ref):
    owner = owner_ref[0, 0]
    core = owner & 1
    across = owner >> 1
    for source, at in ((strip_ref, core), (other_ref, 1 - core)):
        for distance in range(4):
            block = 2 * ((across - distance) & 3) + at
            rows = pl.ds(pl.multiple_of(block * ROWS, ROWS), ROWS)
            for part in range(2):
                out_ref[part, rows, :] = source[distance, part]


def spread_kernel(parts_ref, out_ref):
    total = parts_ref[0]
    for sender in range(1, PARTS):
        total = total + parts_ref[sender]
    out_ref[...] = total


def direction_kernel(first_ref, second_ref, third_ref, fourth_ref, out_ref):
    total = (first_ref[...] + second_ref[...]) + (third_ref[...] + fourth_ref[...])
    direction = total[: 2 * MODES] / jnp.sqrt(total[2 * MODES :] + 1.0)
    for target in range(PARTS):
        out_ref[target] = direction


def assemble_kernel(core_ref, own_ref, other_ref, out_ref):
    core = core_ref[0, 0]
    half = SIDE // 2
    for source, at in ((own_ref, core), (other_ref, 1 - core)):
        base = pl.multiple_of(at * half, half)
        for piece in range(PARTS):
            rows, lanes = place(piece)
            down = pl.ds(pl.multiple_of(base + rows.start, 8), 8)
            for k in range(MODES):
                for part in range(2):
                    out_ref[k, part, down, lanes] = source[piece, 2 * k + part]


VMEM = pl.BlockSpec(memory_space=pltpu.VMEM)
SMEM = pl.BlockSpec(memory_space=pltpu.SMEM)
ANY = pl.BlockSpec(memory_space=pl.ANY)
MIB = 1024 * 1024


def params(mib):
    return pltpu.CompilerParams(vmem_limit_bytes=mib * MIB)


def cost(micros, transcendentals=0):
    return pl.CostEstimate(
        flops=int(micros * 1e9), bytes_accessed=int(1e6), transcendentals=transcendentals
    )


def shape(*sizes):
    return jax.ShapeDtypeStruct(sizes, f32)


def on_device(object_field, probe_modes, amplitudes, positions, shifts):
    forward, slope = tables()
    forward_table = jnp.asarray(two_parts(forward))

    core = lax.axis_index("c")
    core_block = jnp.reshape(core, (1, 1))
    across = lax.axis_index("x")
    owner_block = jnp.reshape(across * 2 + core, (1, 1))
    tiles = 32
    half = SIDE // 2
    cores = [(0, 1), (1, 0)]
    stage = pltpu.VMEM((MODES * SIDE, 2 * WIDE), bf16)
    stage_left = pltpu.VMEM((2 * WIDE, MODES * SIDE), bf16)
    wide = pltpu.VMEM((MODES * SIDE, WIDE), f32)
    tall = pltpu.VMEM((WIDE, MODES * SIDE), f32)
    matrix_left = pltpu.VMEM((WIDE, 3 * WIDE), bf16)
    matrix_right = pltpu.VMEM((3 * WIDE, WIDE), bf16)

    part_rows = lax.dynamic_slice_in_dim(object_field, core * half, half, axis=1)
    near = lax.ppermute(part_rows, TILE, [(i + 1, i) for i in range(tiles - 1)])

    shifted, adjoint = pl.pallas_call(
        probe_kernel,
        out_shape=(shape(MODES, 2, SIDE, SIDE), shape(4, SIDE, SIDE)),
        in_specs=[SMEM, SMEM, VMEM, VMEM],
        out_specs=(VMEM,) * 2,
        scratch_shapes=[stage, stage_left, wide, tall, matrix_right, matrix_left],
        compiler_params=params(22),
        cost_estimate=cost(8, 2048),
    )(positions, shifts, probe_modes, forward_table)

    near, shifted, adjoint = lax.optimization_barrier((near, shifted, adjoint))
    far = lax.ppermute(near, "c", cores)

    piece = shape(PARTS, 2 * MODES + 1, 8, LANES)
    *blocks, staged, mass = pl.pallas_call(
        pattern_kernel,
        out_shape=(shape(2, 3 * ROWS + 8, SIDE),) * 4
        + (jax.ShapeDtypeStruct((MODES * SIDE, 2 * WIDE), bf16), shape(SIDE, SIDE)),
        in_specs=[SMEM, SMEM] + [VMEM] * 6,
        out_specs=(VMEM,) * 6,
        scratch_shapes=[
            stage,
            stage_left,
            wide,
            tall,
            pltpu.VMEM((MODES, 2, SIDE, SIDE), f32),
            pltpu.VMEM((2, SIDE, SIDE), f32),
            matrix_left,
            matrix_right,
            pltpu.VMEM((3, SIDE, SIDE), f32),
        ],
        compiler_params=params(26),
        cost_estimate=cost(8, 65536),
    )(positions, owner_block, object_field, near, far, amplitudes, shifted, forward_table)

    keep, send = pl.pallas_call(
        adjoint_kernel,
        out_shape=(piece, piece),
        in_specs=[SMEM, SMEM] + [VMEM] * 3,
        out_specs=(VMEM,) * 2,
        scratch_shapes=[
            stage_left,
            wide,
            tall,
            matrix_left,
            matrix_right,
            pltpu.VMEM((SIDE, SIDE), f32),
        ],
        compiler_params=params(20),
        cost_estimate=cost(5),
    )(positions, owner_block, staged, mass, adjoint)

    received = [blocks[0]]
    for steps in range(1, 4):
        received.append(lax.ppermute(blocks[steps], "x", [(i, (i + steps) % 4) for i in range(4)]))
    received, send = lax.optimization_barrier((received, send))
    other = lax.ppermute(send, "c", cores)
    received = received + [lax.ppermute(block, "c", cores) for block in received]
    own, spill = pl.pallas_call(
        gather_kernel,
        out_shape=(shape(3, ROWS, 2 * SIDE), shape(3, ROWS, 2 * SIDE)),
        in_specs=[SMEM] + [VMEM] * OWNERS,
        out_specs=(VMEM,) * 2,
        compiler_params=params(8),
        cost_estimate=cost(2),
    )(owner_block, *received)
    summed, own, spill = lax.optimization_barrier((keep + other, own, spill))
    scattered = lax.all_to_all(summed, PLANE, 0, 0)

    shift_grad = pl.pallas_call(
        slope_kernel,
        out_shape=shape(1, 2),
        in_specs=[SMEM] + [VMEM] * 4,
        out_specs=SMEM,
        scratch_shapes=[stage, stage_left, wide, tall, matrix_left, matrix_right],
        compiler_params=params(22),
        cost_estimate=cost(8),
    )(core_block, probe_modes, jnp.asarray(two_parts(slope)), keep, send)

    spilled = lax.ppermute(spill, TILE, [(i, i + 1) for i in range(tiles - 1)])
    updated = pl.pallas_call(
        update_kernel,
        out_shape=shape(2, ROWS, 2 * SIDE),
        in_specs=[SMEM] + [VMEM] * 3,
        out_specs=VMEM,
        compiler_params=params(4),
        cost_estimate=cost(1),
    )(owner_block, object_field, own, spilled)
    scattered, updated, shift_grad = lax.optimization_barrier((scattered, updated, shift_grad))

    def around(value, axis):
        turns = [[(i, (i + step) % 4) for i in range(4)] for step in range(1, 4)]
        return [value] + [lax.ppermute(value, axis, turn) for turn in turns]

    column = pl.pallas_call(
        spread_kernel,
        out_shape=shape(2 * MODES + 1, 8, LANES),
        in_specs=[VMEM],
        out_specs=VMEM,
        compiler_params=params(8),
        cost_estimate=cost(1),
    )(scattered)
    columns = around(column, "zh")
    strip = jnp.stack(around(updated, "x"))
    columns, strip = lax.optimization_barrier((columns, strip))
    direction = pl.pallas_call(
        direction_kernel,
        out_shape=shape(PARTS, 2 * MODES, 8, LANES),
        in_specs=[VMEM] * 4,
        out_specs=VMEM,
        compiler_params=params(4),
        cost_estimate=cost(1, 2048),
    )(*columns)
    spread = lax.all_to_all(direction, PLANE, 0, 0)

    strip_other = lax.ppermute(strip, "c", cores)
    new_object = pl.pallas_call(
        strip_kernel,
        out_shape=shape(2, SIDE, 2 * SIDE),
        in_specs=[SMEM] + [VMEM] * 2,
        out_specs=VMEM,
        compiler_params=params(4),
        cost_estimate=cost(1),
    )(owner_block, strip, strip_other)

    spread, new_object = lax.optimization_barrier((spread, new_object))
    spread_other = lax.ppermute(spread, "c", cores)
    probe_direction = pl.pallas_call(
        assemble_kernel,
        out_shape=shape(MODES, 2, SIDE, SIDE),
        in_specs=[SMEM, VMEM, VMEM],
        out_specs=VMEM,
        compiler_params=params(8),
        cost_estimate=cost(1),
    )(core_block, spread, spread_other)
    return (new_object, probe_direction, shift_grad)


def solution(mesh):
    names = tuple(name for name, _ in AXES)
    sizes = tuple(size for _, size in AXES)
    slice_mesh = Mesh(np.asarray(mesh.devices).reshape(sizes), names)
    return jax.shard_map(
        on_device,
        mesh=slice_mesh,
        in_specs=(
            P(None, TILE, None),
            P(),
            P(names, None, None),
            P(names, None),
            P(names, None),
        ),
        out_specs=(P(None, TILE, None), P(), P(names, None)),
        check_vma=False,
    )
```

```python
import math

import jax
import jax.numpy as jnp
import numpy as np
from jax import lax
from jax.experimental import pallas as pl
from jax.experimental.pallas import tpu as pltpu
from jax.sharding import Mesh
from jax.sharding import PartitionSpec as P

SIDE = 256
MODES = 4
WIDE = 2 * SIDE
full_turn = 2.0 * math.pi
amplitude_floor = 0.5
bf16 = jnp.bfloat16
f32 = jnp.float32

AXES = (("zh", 4), ("zl", 2), ("y", 4), ("x", 4), ("c", 2))
TILE = ("zh", "zl", "y")
BATCH = ("x", "c")
OWNERS = 8
ROWS = SIDE // OWNERS
PLANE = ("zl", "y", "x")
PARTS = 32
LANES = 128


def tables():
    idx = np.arange(SIDE)
    forward = np.exp(-2j * np.pi * (idx[:, None] * idx[None, :] % SIDE) / SIDE) / math.sqrt(SIDE)
    backward = np.conj(forward)
    freq = (((idx + SIDE // 2) % SIDE) - SIDE // 2) / SIDE
    slope = backward @ (freq[:, None] * forward)
    return forward, slope


def two_parts(matrix):
    return np.stack([matrix.real, matrix.imag]).astype(np.float32)


def split(value):
    high = value.astype(bf16)
    low = (value - high.astype(f32)).astype(bf16)
    return high, low


def put_right(stage, row, real, imag):
    rows = slice(row, row + SIDE)
    for at, part in enumerate((real, imag)):
        high, low = split(part)
        stage[rows, at * SIDE : (at + 1) * SIDE] = high
        stage[rows, WIDE + at * SIDE : WIDE + (at + 1) * SIDE] = low


def put_left(stage, col, real, imag):
    cols = slice(col, col + SIDE)
    for at, part in enumerate((real, imag)):
        high, low = split(part)
        stage[at * SIDE : (at + 1) * SIDE, cols] = high
        stage[WIDE + at * SIDE : WIDE + (at + 1) * SIDE, cols] = low


def from_right(stage, matrix):
    fields = jnp.concatenate([stage[...], stage[:, :WIDE]], axis=1)
    return jnp.dot(fields, matrix[...], preferred_element_type=f32)


def from_left(matrix, stage):
    fields = jnp.concatenate([stage[...], stage[:WIDE]], axis=0)
    return jnp.dot(matrix[...], fields, preferred_element_type=f32)


def fill_left(target, real, imag):
    for at, value in enumerate((real, imag)):
        high, low = split(value)
        for third, part in enumerate((high, high, low)):
            base = third * WIDE
            if at == 0:
                target[:SIDE, base : base + SIDE] = part
                target[SIDE:, base + SIDE : base + WIDE] = part
            else:
                target[SIDE:, base : base + SIDE] = part
                target[:SIDE, base + SIDE : base + WIDE] = -part


def fill_right(target, real, imag):
    for at, value in enumerate((real, imag)):
        high, low = split(value)
        for third, part in enumerate((high, high, low)):
            base = third * WIDE
            if at == 0:
                target[base : base + SIDE, :SIDE] = part
                target[base + SIDE : base + WIDE, SIDE:] = part
            else:
                target[base : base + SIDE, SIDE:] = part
                target[base + SIDE : base + WIDE, :SIDE] = -part


def right_to_left(wide, stage_left):
    for k in range(MODES):
        rows = slice(k * SIDE, (k + 1) * SIDE)
        put_left(stage_left, k * SIDE, wide[rows, :SIDE], wide[rows, SIDE:])


def probe_kernel(
    corner_ref,
    shift_ref,
    probe_ref,
    forward_ref,
    shifted_ref,
    adjoint_ref,
    stage,
    stage_left,
    wide,
    tall,
    matrix_right,
    matrix_left,
):
    lane = lax.broadcasted_iota(jnp.int32, (1, SIDE), 1)
    freq = (((lane + SIDE // 2) & (SIDE - 1)) - SIDE // 2).astype(f32) / SIDE

    def ramp(offset, shift):
        whole = ((offset * lane) & (SIDE - 1)).astype(f32) / SIDE
        turns = whole + shift * freq
        angle = -full_turn * (turns - jnp.floor(turns + 0.5))
        return jnp.cos(angle), jnp.sin(angle)

    rows_real, rows_imag = ramp(corner_ref[0, 0], shift_ref[0, 0])
    cols_real, cols_imag = ramp(corner_ref[0, 1], shift_ref[0, 1])
    fwd_real = forward_ref[0]
    fwd_imag = forward_ref[1]
    for at, (real, imag) in enumerate(
        (
            (rows_real, rows_imag),
            (rows_real, -rows_imag),
            (cols_real, cols_imag),
            (cols_real, -cols_imag),
        )
    ):
        put_right(
            stage,
            at * SIDE,
            fwd_real * real + fwd_imag * imag,
            fwd_real * imag - fwd_imag * real,
        )
    fill_right(matrix_right, fwd_real, fwd_imag)
    wide[...] = from_right(stage, matrix_right)
    fill_left(matrix_left, wide[:SIDE, :SIDE], wide[:SIDE, SIDE:])
    adjoint_ref[0] = wide[SIDE : 2 * SIDE, :SIDE]
    adjoint_ref[1] = wide[SIDE : 2 * SIDE, SIDE:]
    adjoint_ref[2] = wide[2 * SIDE : 3 * SIDE, :SIDE]
    adjoint_ref[3] = -wide[2 * SIDE : 3 * SIDE, SIDE:]
    fill_right(matrix_right, wide[3 * SIDE :, :SIDE], -wide[3 * SIDE :, SIDE:])

    for k in range(MODES):
        put_right(stage, k * SIDE, probe_ref[k, 0], probe_ref[k, 1])
    wide[...] = from_right(stage, matrix_right)
    right_to_left(wide, stage_left)
    tall[...] = from_left(matrix_left, stage_left)
    for k in range(MODES):
        cols = slice(k * SIDE, (k + 1) * SIDE)
        shifted_ref[k, 0] = tall[:SIDE, cols]
        shifted_ref[k, 1] = tall[SIDE:, cols]


def partner(owner, steps, turn):
    return (((owner >> 1) + steps) & 3) * 2 + ((owner & 1) ^ turn)


def place(piece):
    row, lane = piece // 2 * 8, piece % 2 * LANES
    return slice(row, row + 8), slice(lane, lane + LANES)


def scatter(target, channel, value):
    for piece in range(PARTS):
        rows, lanes = place(piece)
        target[piece, channel] = value[rows, lanes]


def pattern_kernel(
    corner_ref,
    owner_ref,
    object_ref,
    near_ref,
    far_ref,
    amplitude_ref,
    shifted_ref,
    forward_ref,
    *rest,
):
    block_refs = rest[:4]
    staged_ref, mass_ref = rest[4:6]
    stage, stage_left, wide, tall, exit_wave, patch, left_fwd, right_fwd, nums = rest[6:]
    fill_right(right_fwd, forward_ref[0], forward_ref[1])
    fill_left(left_fwd, forward_ref[0], forward_ref[1])
    owner = owner_ref[0, 0]
    core = owner & 1
    row_start = corner_ref[0, 0] & (SIDE - 1)
    col_start = corner_ref[0, 1]
    row_at = lax.broadcasted_iota(jnp.int32, (SIDE, SIDE), 0)
    col_at = lax.broadcasted_iota(jnp.int32, (SIDE, SIDE), 1)
    here = row_at >= row_start
    left = col_at >= col_start
    first = core == 0
    for part in range(2):
        own = jnp.where(left, object_ref[part, :, :SIDE], object_ref[part, :, SIDE:])
        near = near_ref[part]
        far = far_ref[part]
        rim = jnp.concatenate([jnp.where(first, near, far), jnp.where(first, far, near)], axis=0)
        rim = jnp.where(left, rim[:, :SIDE], rim[:, SIDE:])
        patch[part] = jnp.where(here, own, rim)

    for k in range(MODES):
        real, imag = shifted_ref[k, 0], shifted_ref[k, 1]
        exit_real = real * patch[0] - imag * patch[1]
        exit_imag = real * patch[1] + imag * patch[0]
        exit_wave[k, 0] = exit_real
        exit_wave[k, 1] = exit_imag
        put_right(stage, k * SIDE, exit_real, exit_imag)
    wide[...] = from_right(stage, right_fwd)
    right_to_left(wide, stage_left)
    tall[...] = from_left(left_fwd, stage_left)
    intensity = jnp.zeros((SIDE, SIDE), f32)
    for k in range(MODES):
        cols = slice(k * SIDE, (k + 1) * SIDE)
        real, imag = tall[:SIDE, cols], tall[SIDE:, cols]
        intensity = intensity + (real * real + imag * imag)
    ratio = amplitude_ref[0] / jnp.maximum(jnp.sqrt(intensity), amplitude_floor)
    for k in range(MODES):
        cols = slice(k * SIDE, (k + 1) * SIDE)
        put_left(stage_left, k * SIDE, tall[:SIDE, cols] * ratio, -(tall[SIDE:, cols] * ratio))
    tall[...] = from_left(left_fwd, stage_left)
    for k in range(MODES):
        cols = slice(k * SIDE, (k + 1) * SIDE)
        put_right(stage, k * SIDE, tall[:SIDE, cols], tall[SIDE:, cols])
    wide[...] = from_right(stage, right_fwd)

    num_real = jnp.zeros((SIDE, SIDE), f32)
    num_imag = jnp.zeros((SIDE, SIDE), f32)
    weight = jnp.zeros((SIDE, SIDE), f32)
    for k in range(MODES):
        rows = slice(k * SIDE, (k + 1) * SIDE)
        real, imag = shifted_ref[k, 0], shifted_ref[k, 1]
        change_real = wide[rows, :SIDE] - exit_wave[k, 0]
        change_imag = -wide[rows, SIDE:] - exit_wave[k, 1]
        num_real = num_real + (real * change_real + imag * change_imag)
        num_imag = num_imag + (real * change_imag - imag * change_real)
        weight = weight + (real * real + imag * imag)
        put_right(
            staged_ref,
            k * SIDE,
            patch[0] * change_real + patch[1] * change_imag,
            patch[0] * change_imag - patch[1] * change_real,
        )
    nums[0] = num_real
    nums[1] = num_imag
    nums[2] = weight
    tag = jnp.where(
        lax.broadcasted_iota(jnp.int32, (8, SIDE), 0) == 0, row_start, col_start
    ).astype(f32)
    for steps, block_ref in enumerate(block_refs):
        for turn in range(2):
            base = pl.multiple_of(partner(owner, steps, turn) * ROWS, ROWS)
            for channel in range(3):
                rows = slice(channel * ROWS, (channel + 1) * ROWS)
                block_ref[turn, rows] = nums[channel, pl.ds(base, ROWS), :]
            block_ref[turn, 3 * ROWS :] = tag
    mass_ref[...] = patch[0] * patch[0] + patch[1] * patch[1]


def adjoint_kernel(
    corner_ref,
    owner_ref,
    staged_ref,
    mass_ref,
    adjoint_ref,
    keep_ref,
    send_ref,
    stage_left,
    wide,
    tall,
    matrix_left,
    matrix_right,
    mass,
):
    core = owner_ref[0, 0] & 1
    row_start = corner_ref[0, 0] & (SIDE - 1)
    col_start = corner_ref[0, 1]
    half = SIDE // 2
    fill_right(matrix_right, adjoint_ref[2], adjoint_ref[3])
    wide[...] = from_right(staged_ref, matrix_right)
    fill_left(matrix_left, adjoint_ref[0], adjoint_ref[1])
    right_to_left(wide, stage_left)
    tall[...] = from_left(matrix_left, stage_left)
    turned = pltpu.roll(mass_ref[...], (SIDE - row_start) & (SIDE - 1), 0)
    mass[...] = pltpu.roll(turned, (SIDE - col_start) & (SIDE - 1), 1)
    for target, at in ((keep_ref, core), (send_ref, 1 - core)):
        base = pl.multiple_of(at * half, half)
        for k in range(MODES):
            cols = slice(k * SIDE, (k + 1) * SIDE)
            for part in range(2):
                rows = pl.multiple_of(base + part * SIDE, half)
                scatter(target, 2 * k + part, tall[pl.ds(rows, half), cols])
        scatter(target, 2 * MODES, mass[pl.ds(base, half), :])


def slope_kernel(
    core_ref,
    probe_ref,
    slope_ref,
    keep_ref,
    send_ref,
    shift_grad_ref,
    stage,
    stage_left,
    wide,
    tall,
    matrix_left,
    matrix_right,
):
    first = core_ref[0, 0] == 0
    slope_real = slope_ref[0]
    slope_imag = slope_ref[1]
    fill_left(matrix_left, slope_real, slope_imag)
    fill_right(matrix_right, slope_real.T, slope_imag.T)
    for k in range(MODES):
        put_right(stage, k * SIDE, probe_ref[k, 0], probe_ref[k, 1])
        put_left(stage_left, k * SIDE, probe_ref[k, 0], probe_ref[k, 1])
    tall[...] = from_left(matrix_left, stage_left)
    wide[...] = from_right(stage, matrix_right)
    row_dot = jnp.zeros((8, LANES), f32)
    col_dot = jnp.zeros((8, LANES), f32)
    for piece in range(2 * PARTS):
        top = piece < PARTS
        rows, lanes = place(piece)
        for k in range(MODES):
            kept = [keep_ref[piece % PARTS, 2 * k + part] for part in range(2)]
            sent = [send_ref[piece % PARTS, 2 * k + part] for part in range(2)]
            real, imag = [
                jnp.where(first, a, b) if top else jnp.where(first, b, a)
                for a, b in zip(kept, sent)
            ]
            down = slice(rows.start + SIDE, rows.stop + SIDE)
            over = slice(lanes.start + k * SIDE, lanes.stop + k * SIDE)
            across = slice(rows.start + k * SIDE, rows.stop + k * SIDE)
            wider = slice(lanes.start + SIDE, lanes.stop + SIDE)
            row_dot = row_dot + (real * tall[down, over] - imag * tall[rows, over])
            col_dot = col_dot + (real * wide[across, wider] - imag * wide[across, lanes])
    shift_grad_ref[0, 0] = full_turn / SIDE * jnp.sum(row_dot)
    shift_grad_ref[0, 1] = full_turn / SIDE * jnp.sum(col_dot)


def gather_kernel(owner_ref, *rest):
    own_ref, spill_ref = rest[OWNERS:]
    base = owner_ref[0, 0] * ROWS
    row_at = (base + lax.broadcasted_iota(jnp.int32, (ROWS, SIDE), 0)).astype(f32)
    col_at = lax.broadcasted_iota(jnp.int32, (ROWS, SIDE), 1).astype(f32)
    sums = [[jnp.zeros((ROWS, SIDE), f32) for _ in range(4)] for _ in range(3)]
    for sender in range(OWNERS):
        block_ref = rest[sender].at[sender // 4]
        here = row_at >= block_ref[3 * ROWS : 3 * ROWS + 1]
        left = col_at >= block_ref[3 * ROWS + 1 : 3 * ROWS + 2]
        values = [block_ref[channel * ROWS : (channel + 1) * ROWS] for channel in range(3)]
        for channel, value in enumerate(values):
            value_here = jnp.where(here, value, 0.0)
            value_next = jnp.where(here, 0.0, value)
            terms = (
                jnp.where(left, value_here, 0.0),
                jnp.where(left, 0.0, value_here),
                jnp.where(left, value_next, 0.0),
                jnp.where(left, 0.0, value_next),
            )
            sums[channel] = [total + term for total, term in zip(sums[channel], terms)]
    for channel in range(3):
        own_ref[channel, :, :SIDE] = sums[channel][0]
        own_ref[channel, :, SIDE:] = sums[channel][1]
        spill_ref[channel, :, :SIDE] = sums[channel][2]
        spill_ref[channel, :, SIDE:] = sums[channel][3]


def update_kernel(owner_ref, object_ref, own_ref, spilled_ref, out_ref):
    rows = pl.ds(pl.multiple_of(owner_ref[0, 0] * ROWS, ROWS), ROWS)
    weight = own_ref[2] + spilled_ref[2] + 1.0
    for part in range(2):
        out_ref[part] = object_ref[part, rows, :] + (own_ref[part] + spilled_ref[part]) / weight


def strip_kernel(owner_ref, strip_ref, other_ref, out_ref):
    owner = owner_ref[0, 0]
    core = owner & 1
    across = owner >> 1
    for source, at in ((strip_ref, core), (other_ref, 1 - core)):
        for distance in range(4):
            block = 2 * ((across - distance) & 3) + at
            rows = pl.ds(pl.multiple_of(block * ROWS, ROWS), ROWS)
            for part in range(2):
                out_ref[part, rows, :] = source[distance, part]


def spread_kernel(parts_ref, out_ref):
    total = parts_ref[0]
    for sender in range(1, PARTS):
        total = total + parts_ref[sender]
    out_ref[...] = total


def direction_kernel(first_ref, second_ref, third_ref, fourth_ref, out_ref):
    total = (first_ref[...] + second_ref[...]) + (third_ref[...] + fourth_ref[...])
    direction = total[: 2 * MODES] / jnp.sqrt(total[2 * MODES :] + 1.0)
    for target in range(PARTS):
        out_ref[target] = direction


def assemble_kernel(core_ref, own_ref, other_ref, out_ref):
    core = core_ref[0, 0]
    half = SIDE // 2
    for source, at in ((own_ref, core), (other_ref, 1 - core)):
        base = pl.multiple_of(at * half, half)
        for piece in range(PARTS):
            rows, lanes = place(piece)
            down = pl.ds(pl.multiple_of(base + rows.start, 8), 8)
            for k in range(MODES):
                for part in range(2):
                    out_ref[k, part, down, lanes] = source[piece, 2 * k + part]


VMEM = pl.BlockSpec(memory_space=pltpu.VMEM)
SMEM = pl.BlockSpec(memory_space=pltpu.SMEM)
ANY = pl.BlockSpec(memory_space=pl.ANY)
MIB = 1024 * 1024


def params(mib):
    return pltpu.CompilerParams(vmem_limit_bytes=mib * MIB)


def cost(micros, transcendentals=0):
    return pl.CostEstimate(
        flops=int(micros * 1e9), bytes_accessed=int(1e6), transcendentals=transcendentals
    )


def shape(*sizes):
    return jax.ShapeDtypeStruct(sizes, f32)


def on_device(object_field, probe_modes, amplitudes, positions, shifts):
    forward, slope = tables()
    forward_table = jnp.asarray(two_parts(forward))

    core = lax.axis_index("c")
    core_block = jnp.reshape(core, (1, 1))
    across = lax.axis_index("x")
    owner_block = jnp.reshape(across * 2 + core, (1, 1))
    tiles = 32
    half = SIDE // 2
    cores = [(0, 1), (1, 0)]
    stage = pltpu.VMEM((MODES * SIDE, 2 * WIDE), bf16)
    stage_left = pltpu.VMEM((2 * WIDE, MODES * SIDE), bf16)
    wide = pltpu.VMEM((MODES * SIDE, WIDE), f32)
    tall = pltpu.VMEM((WIDE, MODES * SIDE), f32)
    matrix_left = pltpu.VMEM((WIDE, 3 * WIDE), bf16)
    matrix_right = pltpu.VMEM((3 * WIDE, WIDE), bf16)

    part_rows = lax.dynamic_slice_in_dim(object_field, core * half, half, axis=1)
    near = lax.ppermute(part_rows, TILE, [(i + 1, i) for i in range(tiles - 1)])

    shifted, adjoint = pl.pallas_call(
        probe_kernel,
        out_shape=(shape(MODES, 2, SIDE, SIDE), shape(4, SIDE, SIDE)),
        in_specs=[SMEM, SMEM, VMEM, VMEM],
        out_specs=(VMEM,) * 2,
        scratch_shapes=[stage, stage_left, wide, tall, matrix_right, matrix_left],
        compiler_params=params(22),
        cost_estimate=cost(8, 2048),
    )(positions, shifts, probe_modes, forward_table)

    near, shifted, adjoint = lax.optimization_barrier((near, shifted, adjoint))
    far = lax.ppermute(near, "c", cores)

    piece = shape(PARTS, 2 * MODES + 1, 8, LANES)
    *blocks, staged, mass = pl.pallas_call(
        pattern_kernel,
        out_shape=(shape(2, 3 * ROWS + 8, SIDE),) * 4
        + (jax.ShapeDtypeStruct((MODES * SIDE, 2 * WIDE), bf16), shape(SIDE, SIDE)),
        in_specs=[SMEM, SMEM] + [VMEM] * 6,
        out_specs=(VMEM,) * 6,
        scratch_shapes=[
            stage,
            stage_left,
            wide,
            tall,
            pltpu.VMEM((MODES, 2, SIDE, SIDE), f32),
            pltpu.VMEM((2, SIDE, SIDE), f32),
            matrix_left,
            matrix_right,
            pltpu.VMEM((3, SIDE, SIDE), f32),
        ],
        compiler_params=params(26),
        cost_estimate=cost(8, 65536),
    )(positions, owner_block, object_field, near, far, amplitudes, shifted, forward_table)

    keep, send = pl.pallas_call(
        adjoint_kernel,
        out_shape=(piece, piece),
        in_specs=[SMEM, SMEM] + [VMEM] * 3,
        out_specs=(VMEM,) * 2,
        scratch_shapes=[
            stage_left,
            wide,
            tall,
            matrix_left,
            matrix_right,
            pltpu.VMEM((SIDE, SIDE), f32),
        ],
        compiler_params=params(20),
        cost_estimate=cost(5),
    )(positions, owner_block, staged, mass, adjoint)

    received = [blocks[0]]
    for steps in range(1, 4):
        received.append(lax.ppermute(blocks[steps], "x", [(i, (i + steps) % 4) for i in range(4)]))
    other = lax.ppermute(send, "c", cores)
    received = received + [lax.ppermute(block, "c", cores) for block in received]
    own, spill = pl.pallas_call(
        gather_kernel,
        out_shape=(shape(3, ROWS, 2 * SIDE), shape(3, ROWS, 2 * SIDE)),
        in_specs=[SMEM] + [VMEM] * OWNERS,
        out_specs=(VMEM,) * 2,
        compiler_params=params(8),
        cost_estimate=cost(12),
    )(owner_block, *received)
    summed = keep + other
    scattered = lax.all_to_all(summed, PLANE, 0, 0)

    shift_grad = pl.pallas_call(
        slope_kernel,
        out_shape=shape(1, 2),
        in_specs=[SMEM] + [VMEM] * 4,
        out_specs=SMEM,
        scratch_shapes=[stage, stage_left, wide, tall, matrix_left, matrix_right],
        compiler_params=params(22),
        cost_estimate=cost(8),
    )(core_block, probe_modes, jnp.asarray(two_parts(slope)), keep, send)

    spilled = lax.ppermute(spill, TILE, [(i, i + 1) for i in range(tiles - 1)])
    updated = pl.pallas_call(
        update_kernel,
        out_shape=shape(2, ROWS, 2 * SIDE),
        in_specs=[SMEM] + [VMEM] * 3,
        out_specs=VMEM,
        compiler_params=params(4),
        cost_estimate=cost(1),
    )(owner_block, object_field, own, spilled)
    scattered, updated, shift_grad = lax.optimization_barrier((scattered, updated, shift_grad))

    def around(value, axis):
        turns = [[(i, (i + step) % 4) for i in range(4)] for step in range(1, 4)]
        return [value] + [lax.ppermute(value, axis, turn) for turn in turns]

    column = pl.pallas_call(
        spread_kernel,
        out_shape=shape(2 * MODES + 1, 8, LANES),
        in_specs=[VMEM],
        out_specs=VMEM,
        compiler_params=params(8),
        cost_estimate=cost(1),
    )(scattered)
    columns = around(column, "zh")
    columns, updated = lax.optimization_barrier((columns, updated))
    direction = pl.pallas_call(
        direction_kernel,
        out_shape=shape(PARTS, 2 * MODES, 8, LANES),
        in_specs=[VMEM] * 4,
        out_specs=VMEM,
        compiler_params=params(4),
        cost_estimate=cost(1, 2048),
    )(*columns)
    spread = lax.all_to_all(direction, PLANE, 0, 0)

    strip = jnp.stack(around(updated, "x"))
    strip_other = lax.ppermute(strip, "c", cores)
    new_object = pl.pallas_call(
        strip_kernel,
        out_shape=shape(2, SIDE, 2 * SIDE),
        in_specs=[SMEM] + [VMEM] * 2,
        out_specs=VMEM,
        compiler_params=params(4),
        cost_estimate=cost(15),
    )(owner_block, strip, strip_other)

    spread, new_object = lax.optimization_barrier((spread, new_object))
    spread_other = lax.ppermute(spread, "c", cores)
    probe_direction = pl.pallas_call(
        assemble_kernel,
        out_shape=shape(MODES, 2, SIDE, SIDE),
        in_specs=[SMEM, VMEM, VMEM],
        out_specs=VMEM,
        compiler_params=params(8),
        cost_estimate=cost(1),
    )(core_block, spread, spread_other)
    return (new_object, probe_direction, shift_grad)


def solution(mesh):
    names = tuple(name for name, _ in AXES)
    sizes = tuple(size for _, size in AXES)
    slice_mesh = Mesh(np.asarray(mesh.devices).reshape(sizes), names)
    return jax.shard_map(
        on_device,
        mesh=slice_mesh,
        in_specs=(
            P(None, TILE, None),
            P(),
            P(names, None, None),
            P(names, None),
            P(names, None),
        ),
        out_specs=(P(None, TILE, None), P(), P(names, None)),
        check_vma=False,
    )
```

```python
import math

import jax
import jax.numpy as jnp
import numpy as np
from jax import lax
from jax.experimental import pallas as pl
from jax.experimental.pallas import tpu as pltpu
from jax.sharding import Mesh
from jax.sharding import PartitionSpec as P

SIDE = 256
MODES = 4
WIDE = 2 * SIDE
full_turn = 2.0 * math.pi
amplitude_floor = 0.5
bf16 = jnp.bfloat16
f32 = jnp.float32

AXES = (("zh", 4), ("zl", 2), ("y", 4), ("x", 4), ("c", 2))
TILE = ("zh", "zl", "y")
BATCH = ("x", "c")
OWNERS = 8
ROWS = SIDE // OWNERS
PLANE = ("zl", "y", "x")
PARTS = 32
LANES = 128


def tables():
    idx = np.arange(SIDE)
    forward = np.exp(-2j * np.pi * (idx[:, None] * idx[None, :] % SIDE) / SIDE) / math.sqrt(SIDE)
    backward = np.conj(forward)
    freq = (((idx + SIDE // 2) % SIDE) - SIDE // 2) / SIDE
    slope = backward @ (freq[:, None] * forward)
    return forward, slope


def two_parts(matrix):
    return np.stack([matrix.real, matrix.imag]).astype(np.float32)


def split(value):
    high = value.astype(bf16)
    low = (value - high.astype(f32)).astype(bf16)
    return high, low


def put_right(stage, row, real, imag):
    rows = slice(row, row + SIDE)
    for at, part in enumerate((real, imag)):
        high, low = split(part)
        stage[rows, at * SIDE : (at + 1) * SIDE] = high
        stage[rows, WIDE + at * SIDE : WIDE + (at + 1) * SIDE] = low


def put_left(stage, col, real, imag):
    cols = slice(col, col + SIDE)
    for at, part in enumerate((real, imag)):
        high, low = split(part)
        stage[at * SIDE : (at + 1) * SIDE, cols] = high
        stage[WIDE + at * SIDE : WIDE + (at + 1) * SIDE, cols] = low


def from_right(stage, matrix):
    fields = jnp.concatenate([stage[...], stage[:, :WIDE]], axis=1)
    return jnp.dot(fields, matrix[...], preferred_element_type=f32)


def from_left(matrix, stage):
    fields = jnp.concatenate([stage[...], stage[:WIDE]], axis=0)
    return jnp.dot(matrix[...], fields, preferred_element_type=f32)


def fill_left(target, real, imag):
    for at, value in enumerate((real, imag)):
        high, low = split(value)
        for third, part in enumerate((high, high, low)):
            base = third * WIDE
            if at == 0:
                target[:SIDE, base : base + SIDE] = part
                target[SIDE:, base + SIDE : base + WIDE] = part
            else:
                target[SIDE:, base : base + SIDE] = part
                target[:SIDE, base + SIDE : base + WIDE] = -part


def fill_right(target, real, imag):
    for at, value in enumerate((real, imag)):
        high, low = split(value)
        for third, part in enumerate((high, high, low)):
            base = third * WIDE
            if at == 0:
                target[base : base + SIDE, :SIDE] = part
                target[base + SIDE : base + WIDE, SIDE:] = part
            else:
                target[base : base + SIDE, SIDE:] = part
                target[base + SIDE : base + WIDE, :SIDE] = -part


def right_to_left(wide, stage_left):
    for k in range(MODES):
        rows = slice(k * SIDE, (k + 1) * SIDE)
        put_left(stage_left, k * SIDE, wide[rows, :SIDE], wide[rows, SIDE:])


def probe_kernel(
    corner_ref,
    shift_ref,
    probe_ref,
    forward_ref,
    shifted_ref,
    adjoint_ref,
    stage,
    stage_left,
    wide,
    tall,
    matrix_right,
    matrix_left,
):
    lane = lax.broadcasted_iota(jnp.int32, (1, SIDE), 1)
    freq = (((lane + SIDE // 2) & (SIDE - 1)) - SIDE // 2).astype(f32) / SIDE

    def ramp(offset, shift):
        whole = ((offset * lane) & (SIDE - 1)).astype(f32) / SIDE
        turns = whole + shift * freq
        angle = -full_turn * (turns - jnp.floor(turns + 0.5))
        return jnp.cos(angle), jnp.sin(angle)

    rows_real, rows_imag = ramp(corner_ref[0, 0], shift_ref[0, 0])
    cols_real, cols_imag = ramp(corner_ref[0, 1], shift_ref[0, 1])
    fwd_real = forward_ref[0]
    fwd_imag = forward_ref[1]
    for at, (real, imag) in enumerate(
        (
            (rows_real, rows_imag),
            (rows_real, -rows_imag),
            (cols_real, cols_imag),
            (cols_real, -cols_imag),
        )
    ):
        put_right(
            stage,
            at * SIDE,
            fwd_real * real + fwd_imag * imag,
            fwd_real * imag - fwd_imag * real,
        )
    fill_right(matrix_right, fwd_real, fwd_imag)
    wide[...] = from_right(stage, matrix_right)
    fill_left(matrix_left, wide[:SIDE, :SIDE], wide[:SIDE, SIDE:])
    adjoint_ref[0] = wide[SIDE : 2 * SIDE, :SIDE]
    adjoint_ref[1] = wide[SIDE : 2 * SIDE, SIDE:]
    adjoint_ref[2] = wide[2 * SIDE : 3 * SIDE, :SIDE]
    adjoint_ref[3] = -wide[2 * SIDE : 3 * SIDE, SIDE:]
    fill_right(matrix_right, wide[3 * SIDE :, :SIDE], -wide[3 * SIDE :, SIDE:])

    for k in range(MODES):
        put_right(stage, k * SIDE, probe_ref[k, 0], probe_ref[k, 1])
    wide[...] = from_right(stage, matrix_right)
    right_to_left(wide, stage_left)
    tall[...] = from_left(matrix_left, stage_left)
    for k in range(MODES):
        cols = slice(k * SIDE, (k + 1) * SIDE)
        shifted_ref[k, 0] = tall[:SIDE, cols]
        shifted_ref[k, 1] = tall[SIDE:, cols]


def partner(owner, steps, turn):
    return (((owner >> 1) + steps) & 3) * 2 + ((owner & 1) ^ turn)


def place(piece):
    row, lane = piece // 2 * 8, piece % 2 * LANES
    return slice(row, row + 8), slice(lane, lane + LANES)


def scatter(target, channel, value):
    for piece in range(PARTS):
        rows, lanes = place(piece)
        target[piece, channel] = value[rows, lanes]


def pattern_kernel(
    corner_ref,
    owner_ref,
    object_ref,
    near_ref,
    far_ref,
    amplitude_ref,
    shifted_ref,
    forward_ref,
    *rest,
):
    block_refs = rest[:4]
    staged_ref, mass_ref = rest[4:6]
    stage, stage_left, wide, tall, exit_wave, patch, left_fwd, right_fwd, nums = rest[6:]
    fill_right(right_fwd, forward_ref[0], forward_ref[1])
    fill_left(left_fwd, forward_ref[0], forward_ref[1])
    owner = owner_ref[0, 0]
    core = owner & 1
    row_start = corner_ref[0, 0] & (SIDE - 1)
    col_start = corner_ref[0, 1]
    row_at = lax.broadcasted_iota(jnp.int32, (SIDE, SIDE), 0)
    col_at = lax.broadcasted_iota(jnp.int32, (SIDE, SIDE), 1)
    here = row_at >= row_start
    left = col_at >= col_start
    first = core == 0
    for part in range(2):
        own = jnp.where(left, object_ref[part, :, :SIDE], object_ref[part, :, SIDE:])
        near = near_ref[part]
        far = far_ref[part]
        rim = jnp.concatenate([jnp.where(first, near, far), jnp.where(first, far, near)], axis=0)
        rim = jnp.where(left, rim[:, :SIDE], rim[:, SIDE:])
        patch[part] = jnp.where(here, own, rim)

    for k in range(MODES):
        real, imag = shifted_ref[k, 0], shifted_ref[k, 1]
        exit_real = real * patch[0] - imag * patch[1]
        exit_imag = real * patch[1] + imag * patch[0]
        exit_wave[k, 0] = exit_real
        exit_wave[k, 1] = exit_imag
        put_right(stage, k * SIDE, exit_real, exit_imag)
    wide[...] = from_right(stage, right_fwd)
    right_to_left(wide, stage_left)
    tall[...] = from_left(left_fwd, stage_left)
    intensity = jnp.zeros((SIDE, SIDE), f32)
    for k in range(MODES):
        cols = slice(k * SIDE, (k + 1) * SIDE)
        real, imag = tall[:SIDE, cols], tall[SIDE:, cols]
        intensity = intensity + (real * real + imag * imag)
    ratio = amplitude_ref[0] / jnp.maximum(jnp.sqrt(intensity), amplitude_floor)
    for k in range(MODES):
        cols = slice(k * SIDE, (k + 1) * SIDE)
        put_left(stage_left, k * SIDE, tall[:SIDE, cols] * ratio, -(tall[SIDE:, cols] * ratio))
    tall[...] = from_left(left_fwd, stage_left)
    for k in range(MODES):
        cols = slice(k * SIDE, (k + 1) * SIDE)
        put_right(stage, k * SIDE, tall[:SIDE, cols], tall[SIDE:, cols])
    wide[...] = from_right(stage, right_fwd)

    num_real = jnp.zeros((SIDE, SIDE), f32)
    num_imag = jnp.zeros((SIDE, SIDE), f32)
    weight = jnp.zeros((SIDE, SIDE), f32)
    for k in range(MODES):
        rows = slice(k * SIDE, (k + 1) * SIDE)
        real, imag = shifted_ref[k, 0], shifted_ref[k, 1]
        change_real = wide[rows, :SIDE] - exit_wave[k, 0]
        change_imag = -wide[rows, SIDE:] - exit_wave[k, 1]
        num_real = num_real + (real * change_real + imag * change_imag)
        num_imag = num_imag + (real * change_imag - imag * change_real)
        weight = weight + (real * real + imag * imag)
        put_right(
            staged_ref,
            k * SIDE,
            patch[0] * change_real + patch[1] * change_imag,
            patch[0] * change_imag - patch[1] * change_real,
        )
    nums[0] = num_real
    nums[1] = num_imag
    nums[2] = weight
    tag = jnp.where(
        lax.broadcasted_iota(jnp.int32, (8, SIDE), 0) == 0, row_start, col_start
    ).astype(f32)
    for steps, block_ref in enumerate(block_refs):
        for turn in range(2):
            base = pl.multiple_of(partner(owner, steps, turn) * ROWS, ROWS)
            for channel in range(3):
                rows = slice(channel * ROWS, (channel + 1) * ROWS)
                block_ref[turn, rows] = nums[channel, pl.ds(base, ROWS), :]
            block_ref[turn, 3 * ROWS :] = tag
    mass_ref[...] = patch[0] * patch[0] + patch[1] * patch[1]


def adjoint_kernel(
    corner_ref,
    owner_ref,
    staged_ref,
    mass_ref,
    adjoint_ref,
    keep_ref,
    send_ref,
    stage_left,
    wide,
    tall,
    matrix_left,
    matrix_right,
    mass,
):
    core = owner_ref[0, 0] & 1
    row_start = corner_ref[0, 0] & (SIDE - 1)
    col_start = corner_ref[0, 1]
    half = SIDE // 2
    fill_right(matrix_right, adjoint_ref[2], adjoint_ref[3])
    wide[...] = from_right(staged_ref, matrix_right)
    fill_left(matrix_left, adjoint_ref[0], adjoint_ref[1])
    right_to_left(wide, stage_left)
    tall[...] = from_left(matrix_left, stage_left)
    turned = pltpu.roll(mass_ref[...], (SIDE - row_start) & (SIDE - 1), 0)
    mass[...] = pltpu.roll(turned, (SIDE - col_start) & (SIDE - 1), 1)
    for target, at in ((keep_ref, core), (send_ref, 1 - core)):
        base = pl.multiple_of(at * half, half)
        for k in range(MODES):
            cols = slice(k * SIDE, (k + 1) * SIDE)
            for part in range(2):
                rows = pl.multiple_of(base + part * SIDE, half)
                scatter(target, 2 * k + part, tall[pl.ds(rows, half), cols])
        scatter(target, 2 * MODES, mass[pl.ds(base, half), :])


def slope_kernel(
    core_ref,
    probe_ref,
    slope_ref,
    keep_ref,
    send_ref,
    shift_grad_ref,
    stage,
    stage_left,
    wide,
    tall,
    matrix_left,
    matrix_right,
):
    first = core_ref[0, 0] == 0
    slope_real = slope_ref[0]
    slope_imag = slope_ref[1]
    fill_left(matrix_left, slope_real, slope_imag)
    fill_right(matrix_right, slope_real.T, slope_imag.T)
    for k in range(MODES):
        put_right(stage, k * SIDE, probe_ref[k, 0], probe_ref[k, 1])
        put_left(stage_left, k * SIDE, probe_ref[k, 0], probe_ref[k, 1])
    tall[...] = from_left(matrix_left, stage_left)
    wide[...] = from_right(stage, matrix_right)
    row_dot = jnp.zeros((8, LANES), f32)
    col_dot = jnp.zeros((8, LANES), f32)
    for piece in range(2 * PARTS):
        top = piece < PARTS
        rows, lanes = place(piece)
        for k in range(MODES):
            kept = [keep_ref[piece % PARTS, 2 * k + part] for part in range(2)]
            sent = [send_ref[piece % PARTS, 2 * k + part] for part in range(2)]
            real, imag = [
                jnp.where(first, a, b) if top else jnp.where(first, b, a)
                for a, b in zip(kept, sent)
            ]
            down = slice(rows.start + SIDE, rows.stop + SIDE)
            over = slice(lanes.start + k * SIDE, lanes.stop + k * SIDE)
            across = slice(rows.start + k * SIDE, rows.stop + k * SIDE)
            wider = slice(lanes.start + SIDE, lanes.stop + SIDE)
            row_dot = row_dot + (real * tall[down, over] - imag * tall[rows, over])
            col_dot = col_dot + (real * wide[across, wider] - imag * wide[across, lanes])
    shift_grad_ref[0, 0] = full_turn / SIDE * jnp.sum(row_dot)
    shift_grad_ref[0, 1] = full_turn / SIDE * jnp.sum(col_dot)


def gather_kernel(owner_ref, *rest):
    own_ref, spill_ref = rest[OWNERS:]
    base = owner_ref[0, 0] * ROWS
    row_at = (base + lax.broadcasted_iota(jnp.int32, (ROWS, SIDE), 0)).astype(f32)
    col_at = lax.broadcasted_iota(jnp.int32, (ROWS, SIDE), 1).astype(f32)
    sums = [[jnp.zeros((ROWS, SIDE), f32) for _ in range(4)] for _ in range(3)]
    for sender in range(OWNERS):
        block_ref = rest[sender].at[sender // 4]
        here = row_at >= block_ref[3 * ROWS : 3 * ROWS + 1]
        left = col_at >= block_ref[3 * ROWS + 1 : 3 * ROWS + 2]
        values = [block_ref[channel * ROWS : (channel + 1) * ROWS] for channel in range(3)]
        for channel, value in enumerate(values):
            value_here = jnp.where(here, value, 0.0)
            value_next = jnp.where(here, 0.0, value)
            terms = (
                jnp.where(left, value_here, 0.0),
                jnp.where(left, 0.0, value_here),
                jnp.where(left, value_next, 0.0),
                jnp.where(left, 0.0, value_next),
            )
            sums[channel] = [total + term for total, term in zip(sums[channel], terms)]
    for channel in range(3):
        own_ref[channel, :, :SIDE] = sums[channel][0]
        own_ref[channel, :, SIDE:] = sums[channel][1]
        spill_ref[channel, :, :SIDE] = sums[channel][2]
        spill_ref[channel, :, SIDE:] = sums[channel][3]


def update_kernel(owner_ref, object_ref, own_ref, spilled_ref, out_ref):
    rows = pl.ds(pl.multiple_of(owner_ref[0, 0] * ROWS, ROWS), ROWS)
    weight = own_ref[2] + spilled_ref[2] + 1.0
    for part in range(2):
        out_ref[part] = object_ref[part, rows, :] + (own_ref[part] + spilled_ref[part]) / weight


def strip_kernel(owner_ref, strip_ref, other_ref, out_ref):
    owner = owner_ref[0, 0]
    core = owner & 1
    across = owner >> 1
    for source, at in ((strip_ref, core), (other_ref, 1 - core)):
        for distance in range(4):
            block = 2 * ((across - distance) & 3) + at
            rows = pl.ds(pl.multiple_of(block * ROWS, ROWS), ROWS)
            for part in range(2):
                out_ref[part, rows, :] = source[distance, part]


def spread_kernel(parts_ref, out_ref):
    total = parts_ref[0]
    for sender in range(1, PARTS):
        total = total + parts_ref[sender]
    out_ref[...] = total


def direction_kernel(first_ref, second_ref, third_ref, fourth_ref, out_ref):
    total = (first_ref[...] + second_ref[...]) + (third_ref[...] + fourth_ref[...])
    direction = total[: 2 * MODES] / jnp.sqrt(total[2 * MODES :] + 1.0)
    for target in range(PARTS):
        out_ref[target] = direction


def assemble_kernel(core_ref, own_ref, other_ref, out_ref):
    core = core_ref[0, 0]
    half = SIDE // 2
    for source, at in ((own_ref, core), (other_ref, 1 - core)):
        base = pl.multiple_of(at * half, half)
        for piece in range(PARTS):
            rows, lanes = place(piece)
            down = pl.ds(pl.multiple_of(base + rows.start, 8), 8)
            for k in range(MODES):
                for part in range(2):
                    out_ref[k, part, down, lanes] = source[piece, 2 * k + part]


VMEM = pl.BlockSpec(memory_space=pltpu.VMEM)
SMEM = pl.BlockSpec(memory_space=pltpu.SMEM)
ANY = pl.BlockSpec(memory_space=pl.ANY)
MIB = 1024 * 1024


def params(mib):
    return pltpu.CompilerParams(vmem_limit_bytes=mib * MIB)


def cost(micros, transcendentals=0):
    return pl.CostEstimate(
        flops=int(micros * 1e9), bytes_accessed=int(1e6), transcendentals=transcendentals
    )


def shape(*sizes):
    return jax.ShapeDtypeStruct(sizes, f32)


def on_device(object_field, probe_modes, amplitudes, positions, shifts):
    forward, slope = tables()
    forward_table = jnp.asarray(two_parts(forward))

    core = lax.axis_index("c")
    core_block = jnp.reshape(core, (1, 1))
    across = lax.axis_index("x")
    owner_block = jnp.reshape(across * 2 + core, (1, 1))
    tiles = 32
    half = SIDE // 2
    cores = [(0, 1), (1, 0)]
    stage = pltpu.VMEM((MODES * SIDE, 2 * WIDE), bf16)
    stage_left = pltpu.VMEM((2 * WIDE, MODES * SIDE), bf16)
    wide = pltpu.VMEM((MODES * SIDE, WIDE), f32)
    tall = pltpu.VMEM((WIDE, MODES * SIDE), f32)
    matrix_left = pltpu.VMEM((WIDE, 3 * WIDE), bf16)
    matrix_right = pltpu.VMEM((3 * WIDE, WIDE), bf16)

    part_rows = lax.dynamic_slice_in_dim(object_field, core * half, half, axis=1)
    near = lax.ppermute(part_rows, TILE, [(i + 1, i) for i in range(tiles - 1)])

    shifted, adjoint = pl.pallas_call(
        probe_kernel,
        out_shape=(shape(MODES, 2, SIDE, SIDE), shape(4, SIDE, SIDE)),
        in_specs=[SMEM, SMEM, VMEM, VMEM],
        out_specs=(VMEM,) * 2,
        scratch_shapes=[stage, stage_left, wide, tall, matrix_right, matrix_left],
        compiler_params=params(60),
        cost_estimate=cost(8, 2048),
    )(positions, shifts, probe_modes, forward_table)

    near, shifted, adjoint = lax.optimization_barrier((near, shifted, adjoint))
    far = lax.ppermute(near, "c", cores)

    piece = shape(PARTS, 2 * MODES + 1, 8, LANES)
    *blocks, staged, mass = pl.pallas_call(
        pattern_kernel,
        out_shape=(shape(2, 3 * ROWS + 8, SIDE),) * 4
        + (jax.ShapeDtypeStruct((MODES * SIDE, 2 * WIDE), bf16), shape(SIDE, SIDE)),
        in_specs=[SMEM, SMEM] + [VMEM] * 6,
        out_specs=(VMEM,) * 6,
        scratch_shapes=[
            stage,
            stage_left,
            wide,
            tall,
            pltpu.VMEM((MODES, 2, SIDE, SIDE), f32),
            pltpu.VMEM((2, SIDE, SIDE), f32),
            matrix_left,
            matrix_right,
            pltpu.VMEM((3, SIDE, SIDE), f32),
        ],
        compiler_params=params(26),
        cost_estimate=cost(8, 65536),
    )(positions, owner_block, object_field, near, far, amplitudes, shifted, forward_table)

    keep, send = pl.pallas_call(
        adjoint_kernel,
        out_shape=(piece, piece),
        in_specs=[SMEM, SMEM] + [VMEM] * 3,
        out_specs=(VMEM,) * 2,
        scratch_shapes=[
            stage_left,
            wide,
            tall,
            matrix_left,
            matrix_right,
            pltpu.VMEM((SIDE, SIDE), f32),
        ],
        compiler_params=params(20),
        cost_estimate=cost(5),
    )(positions, owner_block, staged, mass, adjoint)

    received = [blocks[0]]
    for steps in range(1, 4):
        received.append(lax.ppermute(blocks[steps], "x", [(i, (i + steps) % 4) for i in range(4)]))
    other = lax.ppermute(send, "c", cores)
    received = received + [lax.ppermute(block, "c", cores) for block in received]
    own, spill = pl.pallas_call(
        gather_kernel,
        out_shape=(shape(3, ROWS, 2 * SIDE), shape(3, ROWS, 2 * SIDE)),
        in_specs=[SMEM] + [VMEM] * OWNERS,
        out_specs=(VMEM,) * 2,
        compiler_params=params(8),
        cost_estimate=cost(12),
    )(owner_block, *received)
    summed = keep + other
    scattered = lax.all_to_all(summed, PLANE, 0, 0)

    shift_grad = pl.pallas_call(
        slope_kernel,
        out_shape=shape(1, 2),
        in_specs=[SMEM] + [VMEM] * 4,
        out_specs=SMEM,
        scratch_shapes=[stage, stage_left, wide, tall, matrix_left, matrix_right],
        compiler_params=params(22),
        cost_estimate=cost(8),
    )(core_block, probe_modes, jnp.asarray(two_parts(slope)), keep, send)

    spilled = lax.ppermute(spill, TILE, [(i, i + 1) for i in range(tiles - 1)])
    updated = pl.pallas_call(
        update_kernel,
        out_shape=shape(2, ROWS, 2 * SIDE),
        in_specs=[SMEM] + [VMEM] * 3,
        out_specs=VMEM,
        compiler_params=params(4),
        cost_estimate=cost(1),
    )(owner_block, object_field, own, spilled)
    scattered, shift_grad = lax.optimization_barrier((scattered, shift_grad))

    def around(value, axis):
        turns = [[(i, (i + step) % 4) for i in range(4)] for step in range(1, 4)]
        return [value] + [lax.ppermute(value, axis, turn) for turn in turns]

    column = pl.pallas_call(
        spread_kernel,
        out_shape=shape(2 * MODES + 1, 8, LANES),
        in_specs=[VMEM],
        out_specs=VMEM,
        compiler_params=params(8),
        cost_estimate=cost(1),
    )(scattered)
    columns = around(column, "zh")
    columns, updated = lax.optimization_barrier((columns, updated))
    direction = pl.pallas_call(
        direction_kernel,
        out_shape=shape(PARTS, 2 * MODES, 8, LANES),
        in_specs=[VMEM] * 4,
        out_specs=VMEM,
        compiler_params=params(4),
        cost_estimate=cost(1, 2048),
    )(*columns)
    spread = lax.all_to_all(direction, PLANE, 0, 0)

    strip = jnp.stack(around(updated, "x"))
    strip_other = lax.ppermute(strip, "c", cores)
    new_object = pl.pallas_call(
        strip_kernel,
        out_shape=shape(2, SIDE, 2 * SIDE),
        in_specs=[SMEM] + [VMEM] * 2,
        out_specs=VMEM,
        compiler_params=params(4),
        cost_estimate=cost(15),
    )(owner_block, strip, strip_other)

    spread, new_object = lax.optimization_barrier((spread, new_object))
    spread_other = lax.ppermute(spread, "c", cores)
    probe_direction = pl.pallas_call(
        assemble_kernel,
        out_shape=shape(MODES, 2, SIDE, SIDE),
        in_specs=[SMEM, VMEM, VMEM],
        out_specs=VMEM,
        compiler_params=params(8),
        cost_estimate=cost(1),
    )(core_block, spread, spread_other)
    return (new_object, probe_direction, shift_grad)


def solution(mesh):
    names = tuple(name for name, _ in AXES)
    sizes = tuple(size for _, size in AXES)
    slice_mesh = Mesh(np.asarray(mesh.devices).reshape(sizes), names)
    return jax.shard_map(
        on_device,
        mesh=slice_mesh,
        in_specs=(
            P(None, TILE, None),
            P(),
            P(names, None, None),
            P(names, None),
            P(names, None),
        ),
        out_specs=(P(None, TILE, None), P(), P(names, None)),
        check_vma=False,
    )
```

```python
import math

import jax
import jax.numpy as jnp
import numpy as np
from jax import lax
from jax.experimental import pallas as pl
from jax.experimental.pallas import tpu as pltpu
from jax.sharding import Mesh
from jax.sharding import PartitionSpec as P

SIDE = 256
MODES = 4
WIDE = 2 * SIDE
full_turn = 2.0 * math.pi
amplitude_floor = 0.5
bf16 = jnp.bfloat16
f32 = jnp.float32

AXES = (("zh", 4), ("zl", 2), ("y", 4), ("x", 4), ("c", 2))
TILE = ("zh", "zl", "y")
BATCH = ("x", "c")
OWNERS = 8
ROWS = SIDE // OWNERS
PLANE = ("zl", "y", "x")
PARTS = 32
LANES = 128


def tables():
    idx = np.arange(SIDE)
    forward = np.exp(-2j * np.pi * (idx[:, None] * idx[None, :] % SIDE) / SIDE) / math.sqrt(SIDE)
    backward = np.conj(forward)
    freq = (((idx + SIDE // 2) % SIDE) - SIDE // 2) / SIDE
    slope = backward @ (freq[:, None] * forward)
    return forward, slope


def two_parts(matrix):
    return np.stack([matrix.real, matrix.imag]).astype(np.float32)


def split(value):
    high = value.astype(bf16)
    low = (value - high.astype(f32)).astype(bf16)
    return high, low


def put_right(stage, row, real, imag):
    rows = slice(row, row + SIDE)
    for at, part in enumerate((real, imag)):
        high, low = split(part)
        stage[rows, at * SIDE : (at + 1) * SIDE] = high
        stage[rows, WIDE + at * SIDE : WIDE + (at + 1) * SIDE] = low


def put_left(stage, col, real, imag):
    cols = slice(col, col + SIDE)
    for at, part in enumerate((real, imag)):
        high, low = split(part)
        stage[at * SIDE : (at + 1) * SIDE, cols] = high
        stage[WIDE + at * SIDE : WIDE + (at + 1) * SIDE, cols] = low


def from_right(stage, matrix):
    fields = jnp.concatenate([stage[...], stage[:, :WIDE]], axis=1)
    return jnp.dot(fields, matrix[...], preferred_element_type=f32)


def from_left(matrix, stage):
    fields = jnp.concatenate([stage[...], stage[:WIDE]], axis=0)
    return jnp.dot(matrix[...], fields, preferred_element_type=f32)


def fill_left(target, real, imag):
    for at, value in enumerate((real, imag)):
        high, low = split(value)
        for third, part in enumerate((high, high, low)):
            base = third * WIDE
            if at == 0:
                target[:SIDE, base : base + SIDE] = part
                target[SIDE:, base + SIDE : base + WIDE] = part
            else:
                target[SIDE:, base : base + SIDE] = part
                target[:SIDE, base + SIDE : base + WIDE] = -part


def fill_right(target, real, imag):
    for at, value in enumerate((real, imag)):
        high, low = split(value)
        for third, part in enumerate((high, high, low)):
            base = third * WIDE
            if at == 0:
                target[base : base + SIDE, :SIDE] = part
                target[base + SIDE : base + WIDE, SIDE:] = part
            else:
                target[base : base + SIDE, SIDE:] = part
                target[base + SIDE : base + WIDE, :SIDE] = -part


def right_to_left(wide, stage_left):
    for k in range(MODES):
        rows = slice(k * SIDE, (k + 1) * SIDE)
        put_left(stage_left, k * SIDE, wide[rows, :SIDE], wide[rows, SIDE:])


def probe_kernel(
    corner_ref,
    shift_ref,
    probe_ref,
    forward_ref,
    slope_ref,
    shifted_ref,
    adjoint_ref,
    slope_rows_ref,
    slope_cols_ref,
    stage,
    stage_left,
    wide,
    tall,
    matrix_right,
    matrix_left,
):
    lane = lax.broadcasted_iota(jnp.int32, (1, SIDE), 1)
    freq = (((lane + SIDE // 2) & (SIDE - 1)) - SIDE // 2).astype(f32) / SIDE

    def ramp(offset, shift):
        whole = ((offset * lane) & (SIDE - 1)).astype(f32) / SIDE
        turns = whole + shift * freq
        angle = -full_turn * (turns - jnp.floor(turns + 0.5))
        return jnp.cos(angle), jnp.sin(angle)

    rows_real, rows_imag = ramp(corner_ref[0, 0], shift_ref[0, 0])
    cols_real, cols_imag = ramp(corner_ref[0, 1], shift_ref[0, 1])
    fwd_real = forward_ref[0]
    fwd_imag = forward_ref[1]
    for at, (real, imag) in enumerate(
        (
            (rows_real, rows_imag),
            (rows_real, -rows_imag),
            (cols_real, cols_imag),
            (cols_real, -cols_imag),
        )
    ):
        put_right(
            stage,
            at * SIDE,
            fwd_real * real + fwd_imag * imag,
            fwd_real * imag - fwd_imag * real,
        )
    fill_right(matrix_right, fwd_real, fwd_imag)
    wide[...] = from_right(stage, matrix_right)
    fill_left(matrix_left, wide[:SIDE, :SIDE], wide[:SIDE, SIDE:])
    adjoint_ref[0] = wide[SIDE : 2 * SIDE, :SIDE]
    adjoint_ref[1] = wide[SIDE : 2 * SIDE, SIDE:]
    adjoint_ref[2] = wide[2 * SIDE : 3 * SIDE, :SIDE]
    adjoint_ref[3] = -wide[2 * SIDE : 3 * SIDE, SIDE:]
    fill_right(matrix_right, wide[3 * SIDE :, :SIDE], -wide[3 * SIDE :, SIDE:])

    for k in range(MODES):
        put_right(stage, k * SIDE, probe_ref[k, 0], probe_ref[k, 1])
    wide[...] = from_right(stage, matrix_right)
    right_to_left(wide, stage_left)
    tall[...] = from_left(matrix_left, stage_left)
    for k in range(MODES):
        cols = slice(k * SIDE, (k + 1) * SIDE)
        shifted_ref[k, 0] = tall[:SIDE, cols]
        shifted_ref[k, 1] = tall[SIDE:, cols]

    slope_real = slope_ref[0]
    slope_imag = slope_ref[1]
    fill_left(matrix_left, slope_real, slope_imag)
    fill_right(matrix_right, slope_real.T, slope_imag.T)
    for k in range(MODES):
        put_left(stage_left, k * SIDE, probe_ref[k, 0], probe_ref[k, 1])
    slope_rows_ref[...] = from_left(matrix_left, stage_left)
    slope_cols_ref[...] = from_right(stage, matrix_right)


def partner(owner, steps, turn):
    return (((owner >> 1) + steps) & 3) * 2 + ((owner & 1) ^ turn)


def place(piece):
    row, lane = piece // 2 * 8, piece % 2 * LANES
    return slice(row, row + 8), slice(lane, lane + LANES)


def scatter(target, channel, value):
    for piece in range(PARTS):
        rows, lanes = place(piece)
        target[piece, channel] = value[rows, lanes]


def pattern_kernel(
    corner_ref,
    owner_ref,
    object_ref,
    near_ref,
    far_ref,
    amplitude_ref,
    shifted_ref,
    forward_ref,
    *rest,
):
    block_refs = rest[:4]
    staged_ref, mass_ref = rest[4:6]
    stage, stage_left, wide, tall, exit_wave, patch, left_fwd, right_fwd, nums = rest[6:]
    fill_right(right_fwd, forward_ref[0], forward_ref[1])
    fill_left(left_fwd, forward_ref[0], forward_ref[1])
    owner = owner_ref[0, 0]
    core = owner & 1
    row_start = corner_ref[0, 0] & (SIDE - 1)
    col_start = corner_ref[0, 1]
    row_at = lax.broadcasted_iota(jnp.int32, (SIDE, SIDE), 0)
    col_at = lax.broadcasted_iota(jnp.int32, (SIDE, SIDE), 1)
    here = row_at >= row_start
    left = col_at >= col_start
    first = core == 0
    for part in range(2):
        own = jnp.where(left, object_ref[part, :, :SIDE], object_ref[part, :, SIDE:])
        near = near_ref[part]
        far = far_ref[part]
        rim = jnp.concatenate([jnp.where(first, near, far), jnp.where(first, far, near)], axis=0)
        rim = jnp.where(left, rim[:, :SIDE], rim[:, SIDE:])
        patch[part] = jnp.where(here, own, rim)

    for k in range(MODES):
        real, imag = shifted_ref[k, 0], shifted_ref[k, 1]
        exit_real = real * patch[0] - imag * patch[1]
        exit_imag = real * patch[1] + imag * patch[0]
        exit_wave[k, 0] = exit_real
        exit_wave[k, 1] = exit_imag
        put_right(stage, k * SIDE, exit_real, exit_imag)
    wide[...] = from_right(stage, right_fwd)
    right_to_left(wide, stage_left)
    tall[...] = from_left(left_fwd, stage_left)
    intensity = jnp.zeros((SIDE, SIDE), f32)
    for k in range(MODES):
        cols = slice(k * SIDE, (k + 1) * SIDE)
        real, imag = tall[:SIDE, cols], tall[SIDE:, cols]
        intensity = intensity + (real * real + imag * imag)
    ratio = amplitude_ref[0] / jnp.maximum(jnp.sqrt(intensity), amplitude_floor)
    for k in range(MODES):
        cols = slice(k * SIDE, (k + 1) * SIDE)
        put_left(stage_left, k * SIDE, tall[:SIDE, cols] * ratio, -(tall[SIDE:, cols] * ratio))
    tall[...] = from_left(left_fwd, stage_left)
    for k in range(MODES):
        cols = slice(k * SIDE, (k + 1) * SIDE)
        put_right(stage, k * SIDE, tall[:SIDE, cols], tall[SIDE:, cols])
    wide[...] = from_right(stage, right_fwd)

    num_real = jnp.zeros((SIDE, SIDE), f32)
    num_imag = jnp.zeros((SIDE, SIDE), f32)
    weight = jnp.zeros((SIDE, SIDE), f32)
    for k in range(MODES):
        rows = slice(k * SIDE, (k + 1) * SIDE)
        real, imag = shifted_ref[k, 0], shifted_ref[k, 1]
        change_real = wide[rows, :SIDE] - exit_wave[k, 0]
        change_imag = -wide[rows, SIDE:] - exit_wave[k, 1]
        num_real = num_real + (real * change_real + imag * change_imag)
        num_imag = num_imag + (real * change_imag - imag * change_real)
        weight = weight + (real * real + imag * imag)
        put_right(
            staged_ref,
            k * SIDE,
            patch[0] * change_real + patch[1] * change_imag,
            patch[0] * change_imag - patch[1] * change_real,
        )
    nums[0] = num_real
    nums[1] = num_imag
    nums[2] = weight
    tag = jnp.where(
        lax.broadcasted_iota(jnp.int32, (8, SIDE), 0) == 0, row_start, col_start
    ).astype(f32)
    for steps, block_ref in enumerate(block_refs):
        for turn in range(2):
            base = pl.multiple_of(partner(owner, steps, turn) * ROWS, ROWS)
            for channel in range(3):
                rows = slice(channel * ROWS, (channel + 1) * ROWS)
                block_ref[turn, rows] = nums[channel, pl.ds(base, ROWS), :]
            block_ref[turn, 3 * ROWS :] = tag
    mass_ref[...] = patch[0] * patch[0] + patch[1] * patch[1]


def adjoint_kernel(
    corner_ref,
    owner_ref,
    staged_ref,
    mass_ref,
    adjoint_ref,
    keep_ref,
    send_ref,
    stage_left,
    wide,
    tall,
    matrix_left,
    matrix_right,
    mass,
):
    core = owner_ref[0, 0] & 1
    row_start = corner_ref[0, 0] & (SIDE - 1)
    col_start = corner_ref[0, 1]
    half = SIDE // 2
    fill_right(matrix_right, adjoint_ref[2], adjoint_ref[3])
    wide[...] = from_right(staged_ref, matrix_right)
    fill_left(matrix_left, adjoint_ref[0], adjoint_ref[1])
    right_to_left(wide, stage_left)
    tall[...] = from_left(matrix_left, stage_left)
    turned = pltpu.roll(mass_ref[...], (SIDE - row_start) & (SIDE - 1), 0)
    mass[...] = pltpu.roll(turned, (SIDE - col_start) & (SIDE - 1), 1)
    for target, at in ((keep_ref, core), (send_ref, 1 - core)):
        base = pl.multiple_of(at * half, half)
        for k in range(MODES):
            cols = slice(k * SIDE, (k + 1) * SIDE)
            for part in range(2):
                rows = pl.multiple_of(base + part * SIDE, half)
                scatter(target, 2 * k + part, tall[pl.ds(rows, half), cols])
        scatter(target, 2 * MODES, mass[pl.ds(base, half), :])


def slope_kernel(core_ref, tall, wide, keep_ref, send_ref, shift_grad_ref):
    first = core_ref[0, 0] == 0
    row_dot = jnp.zeros((8, LANES), f32)
    col_dot = jnp.zeros((8, LANES), f32)
    for piece in range(2 * PARTS):
        top = piece < PARTS
        rows, lanes = place(piece)
        for k in range(MODES):
            kept = [keep_ref[piece % PARTS, 2 * k + part] for part in range(2)]
            sent = [send_ref[piece % PARTS, 2 * k + part] for part in range(2)]
            real, imag = [
                jnp.where(first, a, b) if top else jnp.where(first, b, a)
                for a, b in zip(kept, sent)
            ]
            down = slice(rows.start + SIDE, rows.stop + SIDE)
            over = slice(lanes.start + k * SIDE, lanes.stop + k * SIDE)
            across = slice(rows.start + k * SIDE, rows.stop + k * SIDE)
            wider = slice(lanes.start + SIDE, lanes.stop + SIDE)
            row_dot = row_dot + (real * tall[down, over] - imag * tall[rows, over])
            col_dot = col_dot + (real * wide[across, wider] - imag * wide[across, lanes])
    shift_grad_ref[0, 0] = full_turn / SIDE * jnp.sum(row_dot)
    shift_grad_ref[0, 1] = full_turn / SIDE * jnp.sum(col_dot)


def gather_kernel(owner_ref, *rest):
    own_ref, spill_ref = rest[OWNERS:]
    base = owner_ref[0, 0] * ROWS
    row_at = (base + lax.broadcasted_iota(jnp.int32, (ROWS, SIDE), 0)).astype(f32)
    col_at = lax.broadcasted_iota(jnp.int32, (ROWS, SIDE), 1).astype(f32)
    sums = [[jnp.zeros((ROWS, SIDE), f32) for _ in range(4)] for _ in range(3)]
    for sender in range(OWNERS):
        block_ref = rest[sender].at[sender // 4]
        here = row_at >= block_ref[3 * ROWS : 3 * ROWS + 1]
        left = col_at >= block_ref[3 * ROWS + 1 : 3 * ROWS + 2]
        values = [block_ref[channel * ROWS : (channel + 1) * ROWS] for channel in range(3)]
        for channel, value in enumerate(values):
            value_here = jnp.where(here, value, 0.0)
            value_next = jnp.where(here, 0.0, value)
            terms = (
                jnp.where(left, value_here, 0.0),
                jnp.where(left, 0.0, value_here),
                jnp.where(left, value_next, 0.0),
                jnp.where(left, 0.0, value_next),
            )
            sums[channel] = [total + term for total, term in zip(sums[channel], terms)]
    for channel in range(3):
        own_ref[channel, :, :SIDE] = sums[channel][0]
        own_ref[channel, :, SIDE:] = sums[channel][1]
        spill_ref[channel, :, :SIDE] = sums[channel][2]
        spill_ref[channel, :, SIDE:] = sums[channel][3]


def update_kernel(owner_ref, object_ref, own_ref, spilled_ref, out_ref):
    rows = pl.ds(pl.multiple_of(owner_ref[0, 0] * ROWS, ROWS), ROWS)
    weight = own_ref[2] + spilled_ref[2] + 1.0
    for part in range(2):
        out_ref[part] = object_ref[part, rows, :] + (own_ref[part] + spilled_ref[part]) / weight


def strip_kernel(owner_ref, strip_ref, other_ref, out_ref):
    owner = owner_ref[0, 0]
    core = owner & 1
    across = owner >> 1
    for source, at in ((strip_ref, core), (other_ref, 1 - core)):
        for distance in range(4):
            block = 2 * ((across - distance) & 3) + at
            rows = pl.ds(pl.multiple_of(block * ROWS, ROWS), ROWS)
            for part in range(2):
                out_ref[part, rows, :] = source[distance, part]


def spread_kernel(parts_ref, out_ref):
    total = parts_ref[0]
    for sender in range(1, PARTS):
        total = total + parts_ref[sender]
    out_ref[...] = total


def direction_kernel(first_ref, second_ref, third_ref, fourth_ref, out_ref):
    total = (first_ref[...] + second_ref[...]) + (third_ref[...] + fourth_ref[...])
    direction = total[: 2 * MODES] / jnp.sqrt(total[2 * MODES :] + 1.0)
    for target in range(PARTS):
        out_ref[target] = direction


def assemble_kernel(core_ref, own_ref, other_ref, out_ref):
    core = core_ref[0, 0]
    half = SIDE // 2
    for source, at in ((own_ref, core), (other_ref, 1 - core)):
        base = pl.multiple_of(at * half, half)
        for piece in range(PARTS):
            rows, lanes = place(piece)
            down = pl.ds(pl.multiple_of(base + rows.start, 8), 8)
            for k in range(MODES):
                for part in range(2):
                    out_ref[k, part, down, lanes] = source[piece, 2 * k + part]


VMEM = pl.BlockSpec(memory_space=pltpu.VMEM)
SMEM = pl.BlockSpec(memory_space=pltpu.SMEM)
ANY = pl.BlockSpec(memory_space=pl.ANY)
MIB = 1024 * 1024


def params(mib):
    return pltpu.CompilerParams(vmem_limit_bytes=mib * MIB)


def cost(micros, transcendentals=0):
    return pl.CostEstimate(
        flops=int(micros * 1e9), bytes_accessed=int(1e6), transcendentals=transcendentals
    )


def shape(*sizes):
    return jax.ShapeDtypeStruct(sizes, f32)


def on_device(object_field, probe_modes, amplitudes, positions, shifts):
    forward, slope = tables()
    forward_table = jnp.asarray(two_parts(forward))

    core = lax.axis_index("c")
    core_block = jnp.reshape(core, (1, 1))
    across = lax.axis_index("x")
    owner_block = jnp.reshape(across * 2 + core, (1, 1))
    tiles = 32
    half = SIDE // 2
    cores = [(0, 1), (1, 0)]
    stage = pltpu.VMEM((MODES * SIDE, 2 * WIDE), bf16)
    stage_left = pltpu.VMEM((2 * WIDE, MODES * SIDE), bf16)
    wide = pltpu.VMEM((MODES * SIDE, WIDE), f32)
    tall = pltpu.VMEM((WIDE, MODES * SIDE), f32)
    matrix_left = pltpu.VMEM((WIDE, 3 * WIDE), bf16)
    matrix_right = pltpu.VMEM((3 * WIDE, WIDE), bf16)

    part_rows = lax.dynamic_slice_in_dim(object_field, core * half, half, axis=1)
    near = lax.ppermute(part_rows, TILE, [(i + 1, i) for i in range(tiles - 1)])

    shifted, adjoint, slope_rows, slope_cols = pl.pallas_call(
        probe_kernel,
        out_shape=(shape(MODES, 2, SIDE, SIDE), shape(4, SIDE, SIDE))
        + (shape(WIDE, MODES * SIDE), shape(MODES * SIDE, WIDE)),
        in_specs=[SMEM, SMEM, VMEM, VMEM, VMEM],
        out_specs=(VMEM,) * 4,
        scratch_shapes=[stage, stage_left, wide, tall, matrix_right, matrix_left],
        compiler_params=params(60),
        cost_estimate=cost(8, 2048),
    )(positions, shifts, probe_modes, forward_table, jnp.asarray(two_parts(slope)))

    near, shifted, adjoint = lax.optimization_barrier((near, shifted, adjoint))
    far = lax.ppermute(near, "c", cores)

    piece = shape(PARTS, 2 * MODES + 1, 8, LANES)
    *blocks, staged, mass = pl.pallas_call(
        pattern_kernel,
        out_shape=(shape(2, 3 * ROWS + 8, SIDE),) * 4
        + (jax.ShapeDtypeStruct((MODES * SIDE, 2 * WIDE), bf16), shape(SIDE, SIDE)),
        in_specs=[SMEM, SMEM] + [VMEM] * 6,
        out_specs=(VMEM,) * 6,
        scratch_shapes=[
            stage,
            stage_left,
            wide,
            tall,
            pltpu.VMEM((MODES, 2, SIDE, SIDE), f32),
            pltpu.VMEM((2, SIDE, SIDE), f32),
            matrix_left,
            matrix_right,
            pltpu.VMEM((3, SIDE, SIDE), f32),
        ],
        compiler_params=params(26),
        cost_estimate=cost(8, 65536),
    )(positions, owner_block, object_field, near, far, amplitudes, shifted, forward_table)

    keep, send = pl.pallas_call(
        adjoint_kernel,
        out_shape=(piece, piece),
        in_specs=[SMEM, SMEM] + [VMEM] * 3,
        out_specs=(VMEM,) * 2,
        scratch_shapes=[
            stage_left,
            wide,
            tall,
            matrix_left,
            matrix_right,
            pltpu.VMEM((SIDE, SIDE), f32),
        ],
        compiler_params=params(20),
        cost_estimate=cost(5),
    )(positions, owner_block, staged, mass, adjoint)

    received = [blocks[0]]
    for steps in range(1, 4):
        received.append(lax.ppermute(blocks[steps], "x", [(i, (i + steps) % 4) for i in range(4)]))
    other = lax.ppermute(send, "c", cores)
    received = received + [lax.ppermute(block, "c", cores) for block in received]
    own, spill = pl.pallas_call(
        gather_kernel,
        out_shape=(shape(3, ROWS, 2 * SIDE), shape(3, ROWS, 2 * SIDE)),
        in_specs=[SMEM] + [VMEM] * OWNERS,
        out_specs=(VMEM,) * 2,
        compiler_params=params(8),
        cost_estimate=cost(12),
    )(owner_block, *received)
    summed = keep + other
    scattered = lax.all_to_all(summed, PLANE, 0, 0)

    shift_grad = pl.pallas_call(
        slope_kernel,
        out_shape=shape(1, 2),
        in_specs=[SMEM] + [VMEM] * 4,
        out_specs=SMEM,
        compiler_params=params(12),
        cost_estimate=cost(8),
    )(core_block, slope_rows, slope_cols, keep, send)

    spilled = lax.ppermute(spill, TILE, [(i, i + 1) for i in range(tiles - 1)])
    updated = pl.pallas_call(
        update_kernel,
        out_shape=shape(2, ROWS, 2 * SIDE),
        in_specs=[SMEM] + [VMEM] * 3,
        out_specs=VMEM,
        compiler_params=params(4),
        cost_estimate=cost(1),
    )(owner_block, object_field, own, spilled)
    scattered, shift_grad = lax.optimization_barrier((scattered, shift_grad))

    def around(value, axis):
        turns = [[(i, (i + step) % 4) for i in range(4)] for step in range(1, 4)]
        return [value] + [lax.ppermute(value, axis, turn) for turn in turns]

    column = pl.pallas_call(
        spread_kernel,
        out_shape=shape(2 * MODES + 1, 8, LANES),
        in_specs=[VMEM],
        out_specs=VMEM,
        compiler_params=params(8),
        cost_estimate=cost(1),
    )(scattered)
    columns = around(column, "zh")
    columns, updated = lax.optimization_barrier((columns, updated))
    direction = pl.pallas_call(
        direction_kernel,
        out_shape=shape(PARTS, 2 * MODES, 8, LANES),
        in_specs=[VMEM] * 4,
        out_specs=VMEM,
        compiler_params=params(4),
        cost_estimate=cost(1, 2048),
    )(*columns)
    spread = lax.all_to_all(direction, PLANE, 0, 0)

    strip = jnp.stack(around(updated, "x"))
    strip_other = lax.ppermute(strip, "c", cores)
    new_object = pl.pallas_call(
        strip_kernel,
        out_shape=shape(2, SIDE, 2 * SIDE),
        in_specs=[SMEM] + [VMEM] * 2,
        out_specs=VMEM,
        compiler_params=params(4),
        cost_estimate=cost(15),
    )(owner_block, strip, strip_other)

    spread, new_object = lax.optimization_barrier((spread, new_object))
    spread_other = lax.ppermute(spread, "c", cores)
    probe_direction = pl.pallas_call(
        assemble_kernel,
        out_shape=shape(MODES, 2, SIDE, SIDE),
        in_specs=[SMEM, VMEM, VMEM],
        out_specs=VMEM,
        compiler_params=params(8),
        cost_estimate=cost(1),
    )(core_block, spread, spread_other)
    return (new_object, probe_direction, shift_grad)


def solution(mesh):
    names = tuple(name for name, _ in AXES)
    sizes = tuple(size for _, size in AXES)
    slice_mesh = Mesh(np.asarray(mesh.devices).reshape(sizes), names)
    return jax.shard_map(
        on_device,
        mesh=slice_mesh,
        in_specs=(
            P(None, TILE, None),
            P(),
            P(names, None, None),
            P(names, None),
            P(names, None),
        ),
        out_specs=(P(None, TILE, None), P(), P(names, None)),
        check_vma=False,
    )
```
